32 devices in a mesh: groups: 2 (over x), expert: 4 (over y, core), donor: 4 (over z).
Axes of the slice: x: 2, y: 2, z: 4, core: 2. Of those that a mesh axis runs over, the one named last changes fastest.
Arguments:
- hidden_in: bfloat16 [1024, 4096], P(('groups', 'expert')), parts along dimension 0, may hold values from -6 to 6
- queries: bfloat16 [1024, 4096], P(('groups', 'expert'), 'donor'), parts along dimension 0, may hold values from -39 to 39
- suffix_kv: bfloat16 [1024, 2, 256], P(('groups', 'expert')), parts along dimension 0, may hold values from -12 to 12
- kv_pool: bfloat16 [128, 2, 32, 256], P(('groups', 'expert', 'donor')), parts along dimension 0, may hold values from -12 to 12
- page_table: int32 [8, 16], P('groups'), parts along dimension 0, may hold values from 0 to 63, as said below
- prefix_len: int32 [8], P('groups'), parts along dimension 0, may hold values from 1 to 512, as said below
- out_weight: bfloat16 [4096, 4096], P('donor', 'expert'), may hold values from -0.09375 to 0.09375
- norm_gain: bfloat16 [4096], replicated, may hold values from 0.099609375 to 1.8984375
- expert_ids: int32 [1024, 4], P(('groups', 'expert')), parts along dimension 0, may hold values from 0 to 7, all different within a row; in each aligned block of 128 rows (0 to 127, 128 to 255, ...) at most 80 rows name the same one
- route_probs: float32 [1024, 4], P(('groups', 'expert')), parts along dimension 0, may hold values from 0.05 to 1
- w_gate_up: bfloat16 [16, 4096, 2, 768], P(('expert', 'donor')), may hold values from -0.09375 to 0.09375
- w_down: bfloat16 [16, 768, 4096], P(('expert', 'donor')), may hold values from -0.15625 to 0.15625
Outputs:
- layer_out: bfloat16 [1024, 4096], P(('groups', 'expert'), 'donor'), parts along dimension 0
- head_out: bfloat16 [1024, 4096], P(('groups', 'expert'), 'donor'), parts along dimension 0
The draws below stay inside these ranges and needn't reach their ends.
There are 2 independent parts, one for each index of `groups`. The reference program is written for one: setup_inputs(seed, part) draws one part's arguments, and reference() takes and returns one part's arrays. A program takes and returns all parts, laid end to end along the dimension named above; an argument that names none is the same for every part. Nothing has to cross between parts.
Inputs may be any that keep to these rules, and one draw needn't show every extreme that they name: For every sequence s the values page_table[s, j] // 4 over j are 0 to 15, each once; pages b * 4 to b * 4 + 3 hold one page of every sequence. `prefix_len`: in every draw one sequence has the longest prefix, 512 tokens. `expert_ids`: the 4 experts of a token differ. Among the 128 tokens of one sequence no expert is named by more than 80 tokens, and in some sequence of every draw some expert is named by exactly 80.
All inputs are finite; a program needn't handle non-finite values.
Results may differ from the reference program's by a relative error of at most 0.0056.
Values may be sent and summed in bfloat16 or wider, within the bound.
No kernel may reach another device: no remote copies, remote signals or barrier semaphores. Data moves between devices by JAX's collectives and lax.ppermute only.
A program may use at most 128 MiB of HBM per device.

```python
import math
import jax
import jax.numpy as jnp
import numpy as np
from jax import lax

D = 4096
HD = 128
FFE = 1536
HEADS = 32
KVH = 2
PAGE = 32
SUF = 128
SEQS = 4
TOKENS = 512
MAXP = 16
POOL = 64
EXPERTS = 8
SHARES = 2
TOP = 4
CAPS = 80


def shared_draws(key):
    query_key = jax.random.fold_in(key, 101)
    cache_key = jax.random.fold_in(key, 102)
    queries = 0.5 * jnp.clip(jax.random.normal(query_key, (TOKENS, HEADS, HD), jnp.float32), -6.0, 6.0)
    suffix = 2.0 * jnp.clip(jax.random.normal(cache_key, (TOKENS, KVH, 2 * HD), jnp.float32), -6.0, 6.0)
    return (queries.reshape(TOKENS, HEADS * HD), suffix)


def draw_queries(key, part):
    return shared_draws(key)[0].astype(jnp.bfloat16)


def draw_suffix_kv(key, part):
    return shared_draws(key)[1].astype(jnp.bfloat16)


def permute_rows(base_key, rows_count, length):
    keys_all = jax.random.split(base_key, rows_count)
    return jax.vmap(lambda row_key: jax.random.permutation(row_key, length))(keys_all)


def draw_page_table(key, part):
    owners = permute_rows(jax.random.fold_in(key, 201), SEQS, MAXP)
    local_slots = permute_rows(jax.random.fold_in(key, 202), MAXP, SEQS)
    table = owners * SEQS + local_slots[owners, jnp.arange(SEQS)[:, None]]
    return table.astype(jnp.int32)


def draw_prefix_len(key, part):
    lengths = jax.random.randint(jax.random.fold_in(key, 301), (SEQS,), 1, MAXP * PAGE + 1)
    longest = jax.random.randint(jax.random.fold_in(key, 302), (), 0, SEQS)
    return jnp.where(jnp.arange(SEQS) == longest, MAXP * PAGE, lengths).astype(jnp.int32)


def steps_of(rng, dims, pieces, least, top_value):
    def one(dim, shards_of):
        heights = jax.random.uniform(jax.random.fold_in(jax.random.fold_in(rng, 6), dim), (shards_of,), jnp.float32, least / len(pieces), top_value / len(pieces))
        return jnp.repeat(jnp.exp(heights), dims[dim] // shards_of).reshape((-1,) + (1,) * (len(dims) - dim - 1))

    level = one(*pieces[0])
    for cut in pieces[1:]:
        level = level * one(*cut)
    return level


def assign_block(key, own, number, rows, number_of, top, bound, slope):
    sequence = jax.random.permutation(key, number_of)
    packed, common = portions_of(number_of, rows * top, bound, slope, True), portions_of(number_of, rows * top, bound, slope, False)
    places = jnp.arange(number_of)

    def named(sizes, turn):
        used = int((sizes > 0).sum())
        fixed = max(1, used // 4)
        passed = fixed + (places - fixed + turn * (used - fixed)) % max(1, number_of - fixed)
        return jnp.zeros((number_of,), jnp.int32).at[sequence[jnp.where(places < fixed, places, passed)]].set(jnp.asarray(sizes, jnp.int32))

    sizes = jnp.where(number % 4 == 0, named(packed, number // 4), named(common, number - number // 4 - 1))
    mixed = jax.random.permutation(jax.random.fold_in(own, 3), number_of)
    source_of, receiver = mixed[0:number_of // 2 * 2:2], mixed[1:number_of // 2 * 2:2]
    margin = jnp.minimum(sizes[source_of] - 1, bound - sizes[receiver]) // 2
    margin = jnp.where((source_of == sequence[0]) | (receiver == sequence[0]) | (sizes[receiver] == 0), 0, jnp.maximum(margin, 0))
    passed = jax.random.randint(jax.random.fold_in(own, 4), (number_of // 2,), 0, 1 << 20) % (margin + 1)
    sizes = sizes.at[source_of].add(-passed).at[receiver].add(passed)
    items = jnp.searchsorted(jnp.cumsum(sizes), jnp.arange(rows * top), side="right").astype(jnp.int32)
    listing = items.reshape(top, rows).T
    listing = listing[jax.random.permutation(jax.random.fold_in(own, 1), rows)]
    turn = jax.random.randint(jax.random.fold_in(own, 2), (rows, 1), 0, top)
    return jnp.take_along_axis(listing, (jnp.arange(top)[None, :] + turn) % top, axis=1)


def portions_of(count, total, reach, lean, full):
    loads = [(1 << 20) // math.isqrt(grade ** lean) + 1 for grade in range(1, count + 1)]
    largest = reach if full else min(reach, max(-(-total // count), total * loads[0] // sum(loads)))
    least = 1 if total - largest >= count - 1 else 0
    given, surplus = [largest] + [least] * (count - 1), total - largest - least * (count - 1)
    while surplus > 0:
        free = [i for i in range(1, count) if given[i] < largest] or [i for i in range(1, count) if given[i] < reach]
        whole, remaining = sum([loads[i] for i in free]), surplus
        for i in free:
            extra = min(reach - given[i], max(1, remaining * loads[i] // whole), surplus)
            given[i] = given[i] + extra
            surplus = surplus - extra
    return np.array(given)


def bell_draw(key, extent, scale, most, cuts=(), kind=jnp.bfloat16):
    values = scale * jax.random.normal(key, extent, jnp.float32)
    if cuts:
        values = values * steps_of(key, extent, cuts, -0.22, 0.18)
    return jnp.clip(values, -most, most).astype(kind)


def setup_inputs(seed: int = 0, part: int = 0) -> dict:
    splits = jax.random.split(jax.random.key(seed), 13)
    part_splits = jax.random.split(jax.random.fold_in(splits[12], part), 13)
    hidden_in = bell_draw(part_splits[0], (TOKENS, D), 1.0, 6.0, ((0, 4),))
    queries = draw_queries(jax.random.fold_in(jax.random.fold_in(splits[12], part), 71), part)
    suffix_kv = draw_suffix_kv(jax.random.fold_in(jax.random.fold_in(splits[12], part), 71), part)
    kv_pool = bell_draw(part_splits[3], (POOL, KVH, PAGE, 2 * HD), 2.0, 12.0, ((0, 16),))
    page_table = draw_page_table(jax.random.fold_in(jax.random.fold_in(splits[12], part), 71), part)
    prefix_len = draw_prefix_len(jax.random.fold_in(jax.random.fold_in(splits[12], part), 71), part)
    out_weight = bell_draw(splits[6], (HEADS * HD, D), (HEADS * HD) ** -0.5, 0.09375, ((0, 4), (1, 4)))
    norm_gain = jnp.clip(1.0 + 0.18 * jax.random.normal(splits[7], (D,), jnp.float32), 0.099609375, 1.8984375).astype(jnp.bfloat16)
    expert_ids_keys = jax.random.split(jax.random.fold_in(part_splits[8], 1), TOKENS // SUF)
    expert_ids_turns = jax.random.permutation(jax.random.fold_in(part_splits[8], 3), TOKENS // SUF)
    expert_ids = jax.vmap(lambda own, number: assign_block(jax.random.fold_in(part_splits[8], 2), own, number, SUF, EXPERTS, TOP, CAPS, 2))(expert_ids_keys, expert_ids_turns).reshape((TOKENS, TOP))
    route_probs = jnp.clip(jnp.exp(math.log(1.0) - 2.9957323 * jax.random.uniform(part_splits[9], (TOKENS, TOP), jnp.float32) ** steps_of(part_splits[9], (TOKENS, TOP), ((0, 4),), -0.2, 0.2)), 0.05, 1.0)
    w_gate_up = bell_draw(splits[10], (EXPERTS * SHARES, D, 2, FFE // SHARES), D ** -0.5, 0.09375, ((0, 16),))
    w_down = bell_draw(splits[11], (EXPERTS * SHARES, FFE // SHARES, D), FFE ** -0.5, 0.15625, ((0, 16),))
    return {"hidden_in": hidden_in, "queries": queries, "suffix_kv": suffix_kv, "kv_pool": kv_pool, "page_table": page_table, "prefix_len": prefix_len, "out_weight": out_weight, "norm_gain": norm_gain, "expert_ids": expert_ids, "route_probs": route_probs, "w_gate_up": w_gate_up, "w_down": w_down}


def reference(hidden_in, queries, suffix_kv, kv_pool, page_table, prefix_len, out_weight, norm_gain, expert_ids, route_probs, w_gate_up, w_down):
    group_size = HEADS // KVH
    score_scale = HD ** (-0.5)
    prefix_pos = jnp.arange(MAXP * PAGE, dtype=jnp.int32)
    causal = jnp.arange(SUF, dtype=jnp.int32)[:, None] >= jnp.arange(SUF, dtype=jnp.int32)[None, :]

    def attend(pair_index):
        seq_index = (pair_index // KVH).astype(jnp.int32)
        kv_index = (pair_index % KVH).astype(jnp.int32)
        query_rows = lax.dynamic_slice_in_dim(queries, seq_index * SUF, SUF, 0).reshape(SUF, HEADS, HD)
        query_rows = lax.dynamic_slice_in_dim(query_rows, kv_index * group_size, group_size, 1)
        page_rows = jnp.take(kv_pool, page_table[seq_index], axis=0)
        page_rows = lax.dynamic_index_in_dim(page_rows, kv_index, 1, keepdims=False).reshape(MAXP * PAGE, 2 * HD)
        fresh_pair = lax.dynamic_slice_in_dim(suffix_kv, seq_index * SUF, SUF, 0)
        fresh_pair = lax.dynamic_index_in_dim(fresh_pair, kv_index, 1, keepdims=False)
        keys_all = jnp.concatenate([page_rows[:, :HD], fresh_pair[:, :HD]], axis=0)
        vals_all = jnp.concatenate([page_rows[:, HD:], fresh_pair[:, HD:]], axis=0)
        prefix_seen = jnp.broadcast_to(prefix_pos[None, :] < prefix_len[seq_index], (SUF, MAXP * PAGE))
        visible = jnp.concatenate([prefix_seen, causal], axis=1)
        scores = jnp.einsum('thc,kc->thk', query_rows.astype(jnp.float32), keys_all.astype(jnp.float32)) * score_scale
        scores = jnp.where(visible[:, None, :], scores, -jnp.inf)
        row_top = lax.optimization_barrier(jnp.max(scores, axis=2, keepdims=True))
        exp_scores = jnp.where(visible[:, None, :], jnp.exp(scores - row_top), 0.0)
        row_total = lax.optimization_barrier(jnp.sum(exp_scores, axis=2, keepdims=True))
        weights = exp_scores.astype(jnp.bfloat16)
        mixed_heads = jnp.einsum('thk,kc->thc', weights.astype(jnp.float32), vals_all.astype(jnp.float32)) / row_total
        return mixed_heads.astype(jnp.bfloat16)
    per_pair = lax.map(attend, jnp.arange(SEQS * KVH, dtype=jnp.int32))
    head_out = per_pair.reshape(SEQS, KVH, SUF, group_size, HD).transpose(0, 2, 1, 3, 4).reshape(TOKENS, HEADS * HD)
    attn_proj = jnp.dot(head_out, out_weight, preferred_element_type=jnp.float32)
    resid = (hidden_in.astype(jnp.float32) + attn_proj).astype(jnp.bfloat16)
    resid_f = resid.astype(jnp.float32)
    normed = (resid_f * lax.rsqrt(lax.optimization_barrier(jnp.mean(resid_f * resid_f, axis=1, keepdims=True)) + 1e-06) * norm_gain.astype(jnp.float32)).astype(jnp.bfloat16)
    gates = route_probs / lax.optimization_barrier(jnp.sum(route_probs, axis=1, keepdims=True))
    ids_grid = expert_ids.reshape(SEQS, SUF, TOP)
    counts = lax.optimization_barrier(jnp.sum((ids_grid[..., None] == jnp.arange(EXPERTS, dtype=jnp.int32)).astype(jnp.int32), axis=2))
    before = jnp.cumsum(counts, axis=1) - counts
    slot_index = jnp.take_along_axis(before, ids_grid, axis=2)
    within = (ids_grid * CAPS + slot_index).astype(jnp.int32)
    token_rows = jnp.broadcast_to(jnp.arange(TOKENS, dtype=jnp.int32).reshape(SEQS, SUF, 1) + 1, (SEQS, SUF, TOP))
    seq_rows = jnp.broadcast_to(jnp.arange(SEQS, dtype=jnp.int32)[:, None, None], (SEQS, SUF, TOP))
    source = jnp.zeros((SEQS, EXPERTS * CAPS), jnp.int32).at[seq_rows, within].set(token_rows)
    gate_table = jnp.zeros((SEQS, EXPERTS * CAPS), jnp.float32).at[seq_rows, within].set(gates.reshape(SEQS, SUF, TOP))
    normed_pad = jnp.concatenate([jnp.zeros((1, D), jnp.bfloat16), normed], axis=0)
    block_units = FFE // SHARES

    def expert_step(moe_pad, expert_index):
        pick_rows = lax.dynamic_slice_in_dim(source, expert_index * CAPS, CAPS, 1).reshape(-1)
        slot_gates = lax.dynamic_slice_in_dim(gate_table, expert_index * CAPS, CAPS, 1).reshape(-1)
        rows_in = jnp.take(normed_pad, pick_rows, axis=0)
        up_blocks = lax.dynamic_slice_in_dim(w_gate_up, expert_index * SHARES, SHARES, 0)
        up_full = up_blocks.transpose(1, 2, 0, 3).reshape(D, 2 * FFE)
        down_full = lax.dynamic_slice_in_dim(w_down, expert_index * SHARES, SHARES, 0).reshape(SHARES * block_units, D)
        gate_up = jnp.dot(rows_in, up_full, preferred_element_type=jnp.float32)
        activated = (jax.nn.silu(gate_up[:, :FFE]) * gate_up[:, FFE:]).astype(jnp.bfloat16)
        result = jnp.dot(activated, down_full, preferred_element_type=jnp.float32).astype(jnp.bfloat16)
        moe_pad = moe_pad.at[pick_rows].add(result.astype(jnp.float32) * slot_gates[:, None])
        return (moe_pad, None)
    moe_pad, unused = lax.scan(expert_step, jnp.zeros((TOKENS + 1, D), jnp.float32), jnp.arange(EXPERTS, dtype=jnp.int32))
    layer_out = (resid_f + moe_pad[1:]).astype(jnp.bfloat16)
    return (layer_out, head_out)
```

```python
import jax
import jax.numpy as jnp
from jax import lax
from jax.sharding import PartitionSpec as P


def attention(queries, suffix_kv, kv_pool, page_table, prefix_len):
    n_expert = lax.axis_size("expert")
    n_donor = lax.axis_size("donor")
    expert_index = lax.axis_index("expert")
    donor_index = lax.axis_index("donor")
    seq_count, page_count = page_table.shape
    suffix_len = queries.shape[0]
    kv_heads = suffix_kv.shape[1]
    head_dim = suffix_kv.shape[2] // 2
    page_len = kv_pool.shape[2]
    my_group = donor_index * kv_heads // n_donor
    owner_index = expert_index * n_donor + donor_index
    owner_of = page_table // seq_count
    held_slot = jnp.sum(jnp.where(owner_of == owner_index, page_table % seq_count, 0), axis=1)
    dest_group = jnp.arange(n_donor, dtype=jnp.int32) * kv_heads // n_donor
    wanted = (held_slot[:, None] * kv_heads + dest_group[None, :]).reshape(-1)
    outgoing = jnp.take(
        kv_pool.reshape(seq_count * kv_heads, page_len, 2 * head_dim), wanted, axis=0
    )
    arrived = lax.all_to_all(outgoing, ("expert", "donor"), split_axis=0, concat_axis=0, tiled=True)
    my_owners = lax.dynamic_index_in_dim(owner_of, expert_index, 0, keepdims=False)
    ordered = jnp.take(arrived, my_owners, axis=0).reshape(page_count * page_len, 2 * head_dim)
    prefix_keys = ordered[:, :head_dim]
    prefix_vals = ordered[:, head_dim:]
    score_scale = head_dim ** (-0.5)
    query_heads = queries.reshape(suffix_len, -1, head_dim)
    fresh_pair = lax.dynamic_index_in_dim(suffix_kv, my_group, 1, keepdims=False)
    causal = jnp.arange(suffix_len)[:, None] >= jnp.arange(suffix_len)[None, :]
    fresh_scores = (
        jnp.einsum(
            "thc,uc->thu", query_heads, fresh_pair[:, :head_dim], preferred_element_type=jnp.float32
        )
        * score_scale
    )
    fresh_scores = jnp.where(causal[:, None, :], fresh_scores, -jnp.inf)
    prefix_tokens = lax.dynamic_index_in_dim(prefix_len, expert_index, 0, keepdims=False)
    block_keys = min(1024, page_count * page_len)
    live_blocks = (prefix_tokens + block_keys - 1) // block_keys

    def block_scores(block_index):
        keys_block = lax.dynamic_slice_in_dim(prefix_keys, block_index * block_keys, block_keys, 0)
        raw_scores = (
            jnp.einsum("thc,kc->thk", query_heads, keys_block, preferred_element_type=jnp.float32)
            * score_scale
        )
        visible = block_index * block_keys + jnp.arange(block_keys) < prefix_tokens
        return jnp.where(visible[None, None, :], raw_scores, -jnp.inf)

    def raise_max(block_index, running):
        return jnp.maximum(running, jnp.max(block_scores(block_index), axis=2))

    row_max = lax.fori_loop(0, live_blocks, raise_max, jnp.max(fresh_scores, axis=2))

    def add_block(block_index, loop_state):
        row_total, weighted = loop_state
        exp_scores = jnp.exp(block_scores(block_index) - row_max[:, :, None])
        vals_block = lax.dynamic_slice_in_dim(prefix_vals, block_index * block_keys, block_keys, 0)
        weighted = weighted + jnp.einsum(
            "thk,kc->thc",
            exp_scores.astype(jnp.bfloat16),
            vals_block,
            preferred_element_type=jnp.float32,
        )
        return (row_total + jnp.sum(exp_scores, axis=2), weighted)

    fresh_exp = jnp.exp(fresh_scores - row_max[:, :, None])
    start_state = (
        jnp.sum(fresh_exp, axis=2),
        jnp.einsum(
            "thu,uc->thc",
            fresh_exp.astype(jnp.bfloat16),
            fresh_pair[:, head_dim:],
            preferred_element_type=jnp.float32,
        ),
    )
    row_total, weighted = lax.fori_loop(0, live_blocks, add_block, start_state)
    return (weighted / row_total[:, :, None]).astype(jnp.bfloat16).reshape(suffix_len, -1)


def shards(
    hidden_in,
    queries,
    suffix_kv,
    kv_pool,
    page_table,
    prefix_len,
    out_weight,
    norm_gain,
    expert_ids,
    route_probs,
    w_gate_up,
    w_down,
):
    f32, bf16 = jnp.float32, jnp.bfloat16
    n_expert = lax.axis_size("expert")
    n_donor = lax.axis_size("donor")
    expert_index = lax.axis_index("expert")
    z = lax.axis_index("donor")
    n_rows = n_expert // 2
    y = expert_index // 2
    core = expert_index % 2
    swap = [(i, i ^ 1) for i in range(n_expert)]
    ring = [(i, (i + 1) % n_donor) for i in range(n_donor)]

    def turn(step):
        return [(i, (i + 2 * step) % n_expert) for i in range(n_expert)]

    suffix_len, model_width = hidden_in.shape
    experts_all = 2 * n_expert
    ff_local = w_gate_up.shape[3]
    share_count = n_donor // 2
    my_expert = 2 * expert_index + z // share_count
    pair_cols = model_width // n_rows
    part_rows = n_rows * suffix_len // n_donor
    columns = model_width // n_donor

    gates = route_probs / jnp.sum(route_probs, axis=1, keepdims=True)
    hits = expert_ids[:, :, None] == jnp.arange(experts_all, dtype=jnp.int32)
    gate_table = jnp.sum(jnp.where(hits, gates[:, :, None], 0.0), axis=1)
    all_gates = lax.all_gather(gate_table.T, "expert", axis=0)
    my_gates = lax.dynamic_index_in_dim(all_gates, my_expert, 1, keepdims=False)
    my_gates = my_gates.reshape(n_rows, 2, suffix_len)

    def core_gates(which):
        rows = lax.dynamic_index_in_dim(my_gates, which, 1, keepdims=False)
        return rows.reshape(n_donor, part_rows)

    own_gates, other_gates = core_gates(core), core_gates(1 - core)

    other_weight = lax.ppermute(out_weight, "expert", swap)
    first_weight = jnp.where(core == 0, out_weight, other_weight)
    second_weight = jnp.where(core == 0, other_weight, out_weight)

    part_owner = z * part_rows // suffix_len
    hidden_rows = lax.dynamic_slice_in_dim(
        hidden_in, z * part_rows % suffix_len, part_rows, 0
    )

    def hidden_block(row):
        return lax.dynamic_slice_in_dim(hidden_rows, row * pair_cols, pair_cols, 1)

    hidden_part = hidden_block(y)
    for step in range(1, n_rows):
        got = lax.ppermute(hidden_block((y + step) % n_rows), "expert", turn(step))
        hidden_part = jnp.where((y - step) % n_rows == part_owner, got, hidden_part)

    head_out = attention(queries, suffix_kv, kv_pool, page_table, prefix_len)

    heads = jnp.zeros((n_rows, suffix_len, head_out.shape[1]), bf16)
    heads = lax.dynamic_update_index_in_dim(heads, head_out, y, 0)
    for step in range(1, n_rows):
        got = lax.ppermute(head_out, "expert", turn(step))
        heads = lax.dynamic_update_index_in_dim(heads, got, (y - step) % n_rows, 0)
    heads = heads.reshape(n_rows * suffix_len, -1)
    terms = jnp.concatenate(
        [
            jnp.dot(heads, first_weight, preferred_element_type=f32),
            jnp.dot(heads, second_weight, preferred_element_type=f32),
        ],
        axis=1,
    ).reshape(n_donor, part_rows, pair_cols)

    def term_part(index):
        return lax.dynamic_index_in_dim(terms, index % n_donor, 0, keepdims=False)

    total = term_part(z - 1)
    for step in range(1, n_donor):
        got = lax.ppermute(total.astype(bf16), "donor", ring)
        total = got.astype(f32) + term_part(z - 1 - step)
    current = (total + hidden_part.astype(f32)).astype(bf16)

    gain_f = norm_gain.astype(f32)
    gate_up_weight = w_gate_up[0].reshape(model_width, 2 * ff_local)
    resid_parts, own_act, other_act = [], [], []
    pending = []
    for step in range(n_donor):
        following = lax.ppermute(current, "donor", ring) if step < n_donor - 1 else None
        block = jnp.zeros((part_rows, n_rows, pair_cols), bf16)
        if n_rows == 2:
            got = lax.ppermute(current, "expert", turn(1))
            block = jnp.concatenate(
                [jnp.where(y == 0, current, got), jnp.where(y == 0, got, current)], axis=1
            )
        else:
            block = lax.dynamic_update_index_in_dim(block, current, y, 1)
            for hop in range(1, n_rows):
                got = lax.ppermute(current, "expert", turn(hop))
                block = lax.dynamic_update_index_in_dim(block, got, (y - hop) % n_rows, 1)
            block = block.reshape(part_rows, model_width)
        resid_parts.append(lax.dynamic_slice_in_dim(block, z * columns, columns, 1))
        block_f = block.astype(f32)
        inverse = lax.rsqrt(jnp.mean(block_f * block_f, axis=1, keepdims=True) + 1e-06)
        normed = (block_f * inverse * gain_f[None, :]).astype(bf16)
        other = lax.ppermute(normed, "expert", swap)
        pending.append((step, normed, other))
        if len(pending) == max(1, n_donor // 2):
            rows_in = jnp.concatenate([p[1] for p in pending] + [p[2] for p in pending], axis=0)
            row_gates = jnp.concatenate(
                [
                    lax.dynamic_index_in_dim(table, (z - p[0]) % n_donor, 0, keepdims=False)
                    for table in (own_gates, other_gates)
                    for p in pending
                ]
            )
            gate_up = jnp.dot(rows_in, gate_up_weight, preferred_element_type=f32)
            act = jax.nn.silu(gate_up[:, :ff_local]) * gate_up[:, ff_local:]
            act = (act * row_gates[:, None]).astype(bf16)
            act = act.reshape(2, len(pending), part_rows, ff_local)
            own_act.append(act[0])
            other_act.append(act[1])
            pending = []
        current = following

    def absolute(parts):
        stacked = jnp.concatenate(parts, axis=0)
        return jnp.concatenate(
            [
                lax.dynamic_index_in_dim(stacked, (z - part) % n_donor, 0, keepdims=False)
                for part in range(n_donor)
            ],
            axis=0,
        )

    act_rows = jnp.concatenate([absolute(other_act), absolute(own_act)], axis=0)
    half_rows = n_rows * suffix_len
    resid_all = absolute([p[None] for p in resid_parts])
    resid = lax.dynamic_slice_in_dim(resid_all, y * suffix_len, suffix_len, 0)

    total = None
    for step in range(1, n_donor + 1):
        down = lax.dynamic_slice_in_dim(
            w_down[0], (z - step) % n_donor * columns, columns, 1
        )
        mixed = jnp.dot(act_rows, down, preferred_element_type=f32)
        got = lax.ppermute(mixed[:half_rows].astype(bf16), "expert", swap)
        pair_sum = (mixed[half_rows:] + got.astype(f32)).reshape(n_rows, suffix_len, columns)
        part_sum = lax.dynamic_index_in_dim(pair_sum, y, 0, keepdims=False)
        for hop in range(1, n_rows):
            sent = lax.dynamic_index_in_dim(pair_sum, (y + hop) % n_rows, 0, keepdims=False)
            part_sum = part_sum + lax.ppermute(sent.astype(bf16), "expert", turn(hop)).astype(f32)
        if total is not None:
            part_sum = part_sum + lax.ppermute(total.astype(bf16), "donor", ring).astype(f32)
        total = part_sum
    layer_out = (total + resid.astype(f32)).astype(bf16)
    return (layer_out, head_out)


def solution(mesh):
    in_specs = (
        P(("groups", "expert"), None),
        P(("groups", "expert"), "donor"),
        P(("groups", "expert"), None, None),
        P(("groups", "expert", "donor"), None, None, None),
        P("groups", None),
        P("groups"),
        P("donor", "expert"),
        P(),
        P(("groups", "expert"), None),
        P(("groups", "expert"), None),
        P(("expert", "donor"), None, None, None),
        P(("expert", "donor"), None, None),
    )
    out_specs = (P(("groups", "expert"), "donor"), P(("groups", "expert"), "donor"))
    return jax.shard_map(shards, mesh=mesh, in_specs=in_specs, out_specs=out_specs, check_vma=False)
```

```python
import jax
import jax.numpy as jnp
from jax import lax
from jax.sharding import PartitionSpec as P


def rotation(count, step):
    return [(i, (i + step) % count) for i in range(count)]


def pick(array, index, axis=0):
    return lax.dynamic_index_in_dim(array, index, axis, keepdims=False)


def fetch_pages(kv_pool, page_table, expert_index, z):
    n_expert = lax.axis_size("expert")
    n_donor = lax.axis_size("donor")
    seq_count = page_table.shape[0]
    kv_heads = kv_pool.shape[1]
    owner_of = page_table // seq_count
    mine = expert_index * n_donor + z
    held_slot = jnp.sum(jnp.where(owner_of == mine, page_table % seq_count, 0), axis=1)
    pages = []
    for step in range(n_expert):
        page = pick(kv_pool, pick(held_slot, (expert_index + step) % n_expert))
        pages.append(lax.ppermute(page, "expert", rotation(n_expert, step)) if step else page)
    column = jnp.stack(pages, axis=0)
    arrived = []
    for step in range(n_donor):
        group = (z + step) % n_donor * kv_heads // n_donor
        block = pick(column, group, 1)
        arrived.append(lax.ppermute(block, "donor", rotation(n_donor, step)) if step else block)
    owners = (
        (z - jnp.arange(n_donor))[:, None] % n_donor
        + (expert_index - jnp.arange(n_expert))[None, :] % n_expert * n_donor
    ).reshape(-1)
    my_owner_of = pick(owner_of, expert_index)
    places = jnp.sum(
        jnp.where(owners[:, None] == my_owner_of[None, :], jnp.arange(my_owner_of.shape[0]), 0),
        axis=1,
    )
    return jnp.concatenate(arrived, axis=0), places


def attention(queries, suffix_kv, pages, places, prefix_tokens, my_group):
    suffix_len = queries.shape[0]
    head_dim = suffix_kv.shape[2] // 2
    page_len = pages.shape[1]
    score_scale = head_dim ** (-0.5)
    query_rows = queries.reshape(suffix_len, -1, head_dim)
    fresh_pair = pick(suffix_kv, my_group, 1)
    flat = pages.reshape(-1, 2 * head_dim)
    visible = (places[:, None] * page_len + jnp.arange(page_len) < prefix_tokens).reshape(-1)
    causal = jnp.arange(suffix_len)[:, None] >= jnp.arange(suffix_len)[None, :]

    def scores(keys, seen):
        raw = jnp.einsum("thc,kc->thk", query_rows, keys, preferred_element_type=jnp.float32)
        return jnp.where(seen, raw * score_scale, -jnp.inf)

    fresh_scores = scores(fresh_pair[:, :head_dim], causal[:, None, :])
    page_scores = scores(flat[:, :head_dim], visible[None, None, :])
    row_top = jnp.maximum(
        jnp.max(fresh_scores, axis=2, keepdims=True), jnp.max(page_scores, axis=2, keepdims=True)
    )
    fresh_exp = jnp.exp(fresh_scores - row_top)
    page_exp = jnp.exp(page_scores - row_top)
    row_total = jnp.sum(fresh_exp, axis=2) + jnp.sum(page_exp, axis=2)

    def mix(exps, vals):
        return jnp.einsum(
            "thk,kc->thc", exps.astype(jnp.bfloat16), vals, preferred_element_type=jnp.float32
        )

    weighted = mix(fresh_exp, fresh_pair[:, head_dim:]) + mix(page_exp, flat[:, head_dim:])
    return (weighted / row_total[:, :, None]).astype(jnp.bfloat16).reshape(suffix_len, -1)


def shards(
    hidden_in,
    queries,
    suffix_kv,
    kv_pool,
    page_table,
    prefix_len,
    out_weight,
    norm_gain,
    expert_ids,
    route_probs,
    w_gate_up,
    w_down,
):
    f32, bf16 = jnp.float32, jnp.bfloat16
    n_expert = lax.axis_size("expert")
    n_donor = lax.axis_size("donor")
    expert_index = lax.axis_index("expert")
    z = lax.axis_index("donor")
    n_rows = n_expert // 2
    y = expert_index // 2
    core = expert_index % 2
    swap = [(i, i ^ 1) for i in range(n_expert)]
    ring = rotation(n_donor, 1)

    def turn(step):
        return rotation(n_expert, 2 * step)

    suffix_len, model_width = hidden_in.shape
    experts_all = 2 * n_expert
    ff_local = w_gate_up.shape[3]
    share_count = n_donor // 2
    my_expert = 2 * expert_index + z // share_count
    pair_cols = model_width // n_rows
    part_rows = n_rows * suffix_len // n_donor
    parts_per_seq = suffix_len // part_rows
    columns = model_width // n_donor
    streams = 2 if n_rows <= 2 else 1
    sub_rows = part_rows // streams
    sub_cols = columns // streams
    pieces = 4
    depth = model_width // pieces

    def weight_piece(index):
        piece = w_gate_up[0, index * depth : (index + 1) * depth]
        return piece.reshape(depth, 2 * ff_local)

    pages, places = fetch_pages(kv_pool, page_table, expert_index, z)

    gates = route_probs / jnp.sum(route_probs, axis=1, keepdims=True)
    hits = expert_ids[:, :, None] == jnp.arange(experts_all, dtype=jnp.int32)
    gate_table = jnp.sum(jnp.where(hits, gates[:, :, None], 0.0), axis=1).T
    tables = [gate_table] + [
        lax.ppermute(gate_table, "expert", rotation(n_expert, step)) for step in range(1, n_expert)
    ]
    all_gates = jnp.stack([pick(table, my_expert) for table in tables], axis=0)

    def core_gates(which):
        rows = [pick(all_gates, (expert_index - 2 * r - which) % n_expert) for r in range(n_rows)]
        return jnp.concatenate(rows).reshape(n_donor, part_rows)

    own_gates, other_gates = core_gates(core), core_gates(1 - core)

    other_weight = lax.ppermute(out_weight, "expert", swap)
    pair_weight = jnp.where(
        core == 0,
        jnp.concatenate([out_weight, other_weight], axis=1),
        jnp.concatenate([other_weight, out_weight], axis=1),
    )

    part_owner = z * part_rows // suffix_len
    hidden_rows = lax.dynamic_slice_in_dim(hidden_in, z * part_rows % suffix_len, part_rows, 0)

    def hidden_block(row):
        return lax.dynamic_slice_in_dim(hidden_rows, row * pair_cols, pair_cols, 1)

    hidden_part = hidden_block(y)
    for step in range(1, n_rows):
        got = lax.ppermute(hidden_block((y + step) % n_rows), "expert", turn(step))
        hidden_part = jnp.where((y - step) % n_rows == part_owner, got, hidden_part)

    weights = [weight_piece(index) for index in range(pieces)]
    pages, pair_weight, hidden_part, weights[0], weights[1] = lax.optimization_barrier(
        (pages, pair_weight, hidden_part, weights[0], weights[1])
    )
    head_out = attention(
        queries,
        suffix_kv,
        pages,
        places,
        pick(prefix_len, expert_index),
        z * suffix_kv.shape[1] // n_donor,
    )

    heads = jnp.zeros((n_rows, suffix_len, head_out.shape[1]), bf16)
    heads = lax.dynamic_update_index_in_dim(heads, head_out, y, 0)
    for step in range(1, n_rows):
        got = lax.ppermute(head_out, "expert", turn(step))
        if step == 1:
            got, weights[2] = lax.optimization_barrier((got, weights[2]))
        heads = lax.dynamic_update_index_in_dim(heads, got, (y - step) % n_rows, 0)
    heads = heads.reshape(n_donor, part_rows, -1)
    heads = jnp.concatenate([pick(heads, (z - 1 - step) % n_donor) for step in range(n_donor)])
    terms = jnp.dot(heads, pair_weight, preferred_element_type=f32)
    terms = terms.reshape(n_donor, streams, sub_rows, pair_cols)

    totals = [terms[0, stream] for stream in range(streams)]
    for step in range(1, n_donor):
        for stream in range(streams):
            got = lax.ppermute(totals[stream].astype(bf16), "donor", ring)
            if step == 1 and stream == 0:
                got, weights[3] = lax.optimization_barrier((got, weights[3]))
            totals[stream] = got.astype(f32) + terms[step, stream]
    hidden_part = hidden_part.reshape(streams, sub_rows, pair_cols)
    current = [
        (totals[stream] + hidden_part[stream].astype(f32)).astype(bf16)
        for stream in range(streams)
    ]

    gain_f = norm_gain.astype(f32)
    resid_parts, own_act, other_act = [], [], []
    batch = max(1, n_donor // 2)
    own_rows, other_rows, row_gates = [], [], []
    for step in range(n_donor):
        following = []
        part = (z - step) % n_donor
        for stream in range(streams):
            if step < n_donor - 1:
                following.append(lax.ppermute(current[stream], "donor", ring))
        for stream in range(streams):
            chunk = current[stream]
            gots = [lax.ppermute(chunk, "expert", turn(hop)) for hop in range(1, n_rows)]
            if step == n_donor - 1 and stream == 0 and own_act:
                gots[0], own_act[0], other_act[0] = lax.optimization_barrier(
                    (gots[0], own_act[0], other_act[0])
                )
            if n_rows == 2:
                block = jnp.concatenate(
                    [jnp.where(y == 0, chunk, gots[0]), jnp.where(y == 0, gots[0], chunk)], axis=1
                )
            else:
                block = jnp.zeros((sub_rows, n_rows, pair_cols), bf16)
                block = lax.dynamic_update_index_in_dim(block, chunk, y, 1)
                for hop, got in enumerate(gots, 1):
                    block = lax.dynamic_update_index_in_dim(block, got, (y - hop) % n_rows, 1)
                block = block.reshape(sub_rows, model_width)
            resid_parts.append(lax.dynamic_slice_in_dim(block, z * columns, columns, 1))
            block_f = block.astype(f32)
            inverse = lax.rsqrt(jnp.mean(block_f * block_f, axis=1, keepdims=True) + 1e-06)
            normed = (block_f * inverse * gain_f[None, :]).astype(bf16)
            own_rows.append(normed)
            other_rows.append(lax.ppermute(normed, "expert", swap))
        row_gates.append((pick(own_gates, part), pick(other_gates, part)))
        if len(row_gates) == batch:
            rows_in = jnp.concatenate(own_rows + other_rows, axis=0)
            scale = jnp.concatenate([g[0] for g in row_gates] + [g[1] for g in row_gates])
            gate_up = jnp.dot(rows_in[:, :depth], weights[0], preferred_element_type=f32)
            for index in range(1, pieces):
                gate_up = gate_up + jnp.dot(
                    rows_in[:, index * depth : (index + 1) * depth],
                    weights[index],
                    preferred_element_type=f32,
                )
            act = jax.nn.silu(gate_up[:, :ff_local]) * gate_up[:, ff_local:]
            act = (act * scale[:, None]).astype(bf16).reshape(2, batch, part_rows, ff_local)
            own_act.append(act[0])
            other_act.append(act[1])
            own_rows, other_rows, row_gates = [], [], []
        current = following

    def by_sequence(stacked, rows):
        return jnp.concatenate(
            [
                pick(stacked, (z - (y + r) % n_rows * parts_per_seq - i) % n_donor)
                for r in range(rows)
                for i in range(parts_per_seq)
            ],
            axis=0,
        )

    act_rows = jnp.concatenate(
        [
            by_sequence(jnp.concatenate(other_act, axis=0), n_rows),
            by_sequence(jnp.concatenate(own_act, axis=0), n_rows),
        ],
        axis=0,
    )
    half_rows = n_rows * suffix_len
    resid = by_sequence(
        jnp.concatenate(resid_parts, axis=0).reshape(n_donor, part_rows, columns), 1
    ).astype(f32)

    totals = [None] * streams
    swapped = []
    for step in range(1, n_donor + 1):
        if step >= 3:
            act_rows, swapped[step - 3] = lax.optimization_barrier((act_rows, swapped[step - 3]))
        down = lax.dynamic_slice_in_dim(w_down[0], (z - step) % n_donor * columns, columns, 1)
        mixed = jnp.dot(act_rows, down, preferred_element_type=f32)
        swapped.append(
            [
                lax.ppermute(
                    mixed[:half_rows, stream * sub_cols : (stream + 1) * sub_cols].astype(bf16),
                    "expert",
                    swap,
                )
                for stream in range(streams)
            ]
        )
        swapped[step - 1].append(mixed[half_rows:])
    for step in range(1, n_donor + 1):
        kept = swapped[step - 1][streams]
        for stream in range(streams):
            pair_sum = kept[:, stream * sub_cols : (stream + 1) * sub_cols] + swapped[step - 1][
                stream
            ].astype(f32)
            pair_sum = pair_sum.reshape(n_rows, suffix_len, sub_cols)
            part_sum = pair_sum[0]
            for hop in range(1, n_rows):
                sent = pair_sum[hop].astype(bf16)
                part_sum = part_sum + lax.ppermute(sent, "expert", turn(hop)).astype(f32)
            if totals[stream] is not None:
                last = lax.ppermute(totals[stream].astype(bf16), "donor", ring)
                part_sum = part_sum + last.astype(f32)
            totals[stream] = part_sum
    layer_out = (jnp.concatenate(totals, axis=1) + resid).astype(bf16)
    return (layer_out, head_out)


def solution(mesh):
    in_specs = (
        P(("groups", "expert"), None),
        P(("groups", "expert"), "donor"),
        P(("groups", "expert"), None, None),
        P(("groups", "expert", "donor"), None, None, None),
        P("groups", None),
        P("groups"),
        P("donor", "expert"),
        P(),
        P(("groups", "expert"), None),
        P(("groups", "expert"), None),
        P(("expert", "donor"), None, None, None),
        P(("expert", "donor"), None, None),
    )
    out_specs = (P(("groups", "expert"), "donor"), P(("groups", "expert"), "donor"))
    return jax.shard_map(shards, mesh=mesh, in_specs=in_specs, out_specs=out_specs, check_vma=False)
```

```python
import jax
import jax.numpy as jnp
from jax import lax
from jax.sharding import PartitionSpec as P


def rotation(count, step):
    return [(i, (i + step) % count) for i in range(count)]


def pick(array, index, axis=0):
    return lax.dynamic_index_in_dim(array, index, axis, keepdims=False)


def attention(queries, suffix_kv, kv_pool, page_table, prefix_len, early):
    n_expert = lax.axis_size("expert")
    n_donor = lax.axis_size("donor")
    expert_index = lax.axis_index("expert")
    donor_index = lax.axis_index("donor")
    seq_count, page_count = page_table.shape
    suffix_len = queries.shape[0]
    kv_heads = suffix_kv.shape[1]
    head_dim = suffix_kv.shape[2] // 2
    page_len = kv_pool.shape[2]
    my_group = donor_index * kv_heads // n_donor
    owner_index = expert_index * n_donor + donor_index
    owner_of = page_table // seq_count
    held_slot = jnp.sum(jnp.where(owner_of == owner_index, page_table % seq_count, 0), axis=1)
    dest_group = jnp.arange(n_donor, dtype=jnp.int32) * kv_heads // n_donor
    wanted = (held_slot[:, None] * kv_heads + dest_group[None, :]).reshape(-1)
    outgoing = jnp.take(
        kv_pool.reshape(seq_count * kv_heads, page_len, 2 * head_dim), wanted, axis=0
    )
    arrived = lax.all_to_all(outgoing, ("expert", "donor"), split_axis=0, concat_axis=0, tiled=True)
    arrived, early = lax.optimization_barrier((arrived, early))
    my_owners = lax.dynamic_index_in_dim(owner_of, expert_index, 0, keepdims=False)
    ordered = jnp.take(arrived, my_owners, axis=0).reshape(page_count * page_len, 2 * head_dim)
    prefix_keys = ordered[:, :head_dim]
    prefix_vals = ordered[:, head_dim:]
    score_scale = head_dim ** (-0.5)
    query_heads = queries.reshape(suffix_len, -1, head_dim)
    fresh_pair = lax.dynamic_index_in_dim(suffix_kv, my_group, 1, keepdims=False)
    causal = jnp.arange(suffix_len)[:, None] >= jnp.arange(suffix_len)[None, :]
    fresh_scores = (
        jnp.einsum(
            "thc,uc->thu", query_heads, fresh_pair[:, :head_dim], preferred_element_type=jnp.float32
        )
        * score_scale
    )
    fresh_scores = jnp.where(causal[:, None, :], fresh_scores, -jnp.inf)
    prefix_tokens = lax.dynamic_index_in_dim(prefix_len, expert_index, 0, keepdims=False)
    block_keys = min(1024, page_count * page_len)
    live_blocks = (prefix_tokens + block_keys - 1) // block_keys

    def block_scores(block_index):
        keys_block = lax.dynamic_slice_in_dim(prefix_keys, block_index * block_keys, block_keys, 0)
        raw_scores = (
            jnp.einsum("thc,kc->thk", query_heads, keys_block, preferred_element_type=jnp.float32)
            * score_scale
        )
        visible = block_index * block_keys + jnp.arange(block_keys) < prefix_tokens
        return jnp.where(visible[None, None, :], raw_scores, -jnp.inf)

    def raise_max(block_index, running):
        return jnp.maximum(running, jnp.max(block_scores(block_index), axis=2))

    row_max = lax.fori_loop(0, live_blocks, raise_max, jnp.max(fresh_scores, axis=2))

    def add_block(block_index, loop_state):
        row_total, weighted = loop_state
        exp_scores = jnp.exp(block_scores(block_index) - row_max[:, :, None])
        vals_block = lax.dynamic_slice_in_dim(prefix_vals, block_index * block_keys, block_keys, 0)
        weighted = weighted + jnp.einsum(
            "thk,kc->thc",
            exp_scores.astype(jnp.bfloat16),
            vals_block,
            preferred_element_type=jnp.float32,
        )
        return (row_total + jnp.sum(exp_scores, axis=2), weighted)

    fresh_exp = jnp.exp(fresh_scores - row_max[:, :, None])
    start_state = (
        jnp.sum(fresh_exp, axis=2),
        jnp.einsum(
            "thu,uc->thc",
            fresh_exp.astype(jnp.bfloat16),
            fresh_pair[:, head_dim:],
            preferred_element_type=jnp.float32,
        ),
    )
    row_total, weighted = lax.fori_loop(0, live_blocks, add_block, start_state)
    return (weighted / row_total[:, :, None]).astype(jnp.bfloat16).reshape(suffix_len, -1), early


def shards(
    hidden_in,
    queries,
    suffix_kv,
    kv_pool,
    page_table,
    prefix_len,
    out_weight,
    norm_gain,
    expert_ids,
    route_probs,
    w_gate_up,
    w_down,
):
    f32, bf16 = jnp.float32, jnp.bfloat16
    n_expert = lax.axis_size("expert")
    n_donor = lax.axis_size("donor")
    expert_index = lax.axis_index("expert")
    z = lax.axis_index("donor")
    n_rows = n_expert // 2
    y = expert_index // 2
    core = expert_index % 2
    swap = [(i, i ^ 1) for i in range(n_expert)]

    def turn(step):
        return rotation(n_expert, 2 * step)

    suffix_len, model_width = hidden_in.shape
    experts_all = 2 * n_expert
    ff_local = w_gate_up.shape[3]
    share_count = n_donor // 2
    my_expert = 2 * expert_index + z // share_count
    pair_cols = model_width // n_rows
    part_rows = n_rows * suffix_len // n_donor
    parts_per_seq = suffix_len // part_rows
    columns = model_width // n_donor
    steps = sorted(range(1, n_donor), key=lambda step: min(step, n_donor - step))

    gates = route_probs / jnp.sum(route_probs, axis=1, keepdims=True)
    hits = expert_ids[:, :, None] == jnp.arange(experts_all, dtype=jnp.int32)
    gate_table = jnp.sum(jnp.where(hits, gates[:, :, None], 0.0), axis=1).T
    tables = [gate_table] + [
        lax.ppermute(gate_table, "expert", rotation(n_expert, step)) for step in range(1, n_expert)
    ]

    other_weight = lax.ppermute(out_weight, "expert", swap)

    part_owner = z * part_rows // suffix_len
    hidden_rows = lax.dynamic_slice_in_dim(hidden_in, z * part_rows % suffix_len, part_rows, 0)

    def hidden_block(row):
        return lax.dynamic_slice_in_dim(hidden_rows, row * pair_cols, pair_cols, 1)

    hidden_part = hidden_block(y)
    for step in range(1, n_rows):
        got = lax.ppermute(hidden_block((y + step) % n_rows), "expert", turn(step))
        hidden_part = jnp.where((y - step) % n_rows == part_owner, got, hidden_part)

    head_out, (tables, other_weight, hidden_part) = attention(
        queries,
        suffix_kv,
        kv_pool,
        page_table,
        prefix_len,
        (tables, other_weight, hidden_part),
    )

    heads = jnp.zeros((n_rows, suffix_len, head_out.shape[1]), bf16)
    heads = lax.dynamic_update_index_in_dim(heads, head_out, y, 0)
    for step in range(1, n_rows):
        got = lax.ppermute(head_out, "expert", turn(step))
        heads = lax.dynamic_update_index_in_dim(heads, got, (y - step) % n_rows, 0)
    heads = heads.reshape(n_donor, part_rows, -1)
    heads = jnp.concatenate([pick(heads, (z + step) % n_donor) for step in range(n_donor)])
    own_terms = jnp.dot(heads, out_weight, preferred_element_type=f32)
    other_terms = jnp.dot(heads, other_weight, preferred_element_type=f32)

    def term(step):
        rows = slice(step * part_rows, (step + 1) * part_rows)
        own, other = own_terms[rows], other_terms[rows]
        return jnp.concatenate(
            [jnp.where(core == 0, own, other), jnp.where(core == 0, other, own)], axis=1
        )

    gate_up_weight = w_gate_up[0].reshape(model_width, 2 * ff_local)
    gots = [
        lax.ppermute(term(step).astype(bf16), "donor", rotation(n_donor, step)) for step in steps
    ]
    gots, gate_up_weight = lax.optimization_barrier((gots, gate_up_weight))
    total = term(0) + hidden_part.astype(f32)
    for got in gots:
        total = total + got.astype(f32)
    chunk = total.astype(bf16)

    all_gates = jnp.stack([pick(table, my_expert) for table in tables], axis=0)

    def core_gates(which):
        rows = [pick(all_gates, (expert_index - 2 * r - which) % n_expert) for r in range(n_rows)]
        return jnp.concatenate(rows).reshape(n_donor, part_rows)

    own_gates, other_gates = core_gates(core), core_gates(1 - core)

    gain_f = norm_gain.astype(f32)
    chunks = [chunk] + [lax.ppermute(chunk, "donor", rotation(n_donor, step)) for step in steps]
    slots = [0] + steps
    resid_parts = [None] * n_donor
    own_act, other_act = [None] * n_donor, [None] * n_donor
    batch = max(1, n_donor // 2)
    own_rows, other_rows, row_gates = [], [], []
    for place, (slot, chunk) in enumerate(zip(slots, chunks)):
        part = (z - slot) % n_donor
        gots = [lax.ppermute(chunk, "expert", turn(hop)) for hop in range(1, n_rows)]
        if place == n_donor - 1 and place >= batch and gots:
            early = [slots[i] for i in range(batch)]
            gots, acts = lax.optimization_barrier(
                (gots, [(own_act[i], other_act[i]) for i in early])
            )
            for i, pair in zip(early, acts):
                own_act[i], other_act[i] = pair
        if n_rows == 2:
            block = jnp.concatenate(
                [jnp.where(y == 0, chunk, gots[0]), jnp.where(y == 0, gots[0], chunk)], axis=1
            )
        else:
            block = jnp.zeros((part_rows, n_rows, pair_cols), bf16)
            block = lax.dynamic_update_index_in_dim(block, chunk, y, 1)
            for hop, got in enumerate(gots, 1):
                block = lax.dynamic_update_index_in_dim(block, got, (y - hop) % n_rows, 1)
            block = block.reshape(part_rows, model_width)
        resid_parts[slot] = lax.dynamic_slice_in_dim(block, z * columns, columns, 1)
        block_f = block.astype(f32)
        inverse = lax.rsqrt(jnp.mean(block_f * block_f, axis=1, keepdims=True) + 1e-06)
        normed = (block_f * inverse * gain_f[None, :]).astype(bf16)
        own_rows.append(normed)
        other_rows.append(lax.ppermute(normed, "expert", swap))
        row_gates.append((pick(own_gates, part), pick(other_gates, part)))
        if len(row_gates) == batch:
            rows_in = jnp.concatenate(own_rows + other_rows, axis=0)
            scale = jnp.concatenate([g[0] for g in row_gates] + [g[1] for g in row_gates])
            gate_up = jnp.dot(rows_in, gate_up_weight, preferred_element_type=f32)
            act = jax.nn.silu(gate_up[:, :ff_local]) * gate_up[:, ff_local:]
            act = (act * scale[:, None]).astype(bf16).reshape(2, batch, part_rows, ff_local)
            for i in range(batch):
                own_act[slots[place - batch + 1 + i]] = act[0, i]
                other_act[slots[place - batch + 1 + i]] = act[1, i]
            own_rows, other_rows, row_gates = [], [], []

    def by_sequence(parts, rows):
        stacked = jnp.stack(parts, axis=0)
        return jnp.concatenate(
            [
                pick(stacked, (z - (y + r) % n_rows * parts_per_seq - i) % n_donor)
                for r in range(rows)
                for i in range(parts_per_seq)
            ],
            axis=0,
        )

    act_rows = jnp.concatenate(
        [by_sequence(other_act, n_rows), by_sequence(own_act, n_rows)], axis=0
    )
    half_rows = n_rows * suffix_len
    resid = by_sequence(resid_parts, 1).astype(f32)

    swapped, kept = [], []
    order = steps[::-1] + [0]
    for place, step in enumerate(order):
        if place >= 2:
            act_rows, swapped[place - 2] = lax.optimization_barrier((act_rows, swapped[place - 2]))
        down = lax.dynamic_slice_in_dim(w_down[0], (z + step) % n_donor * columns, columns, 1)
        mixed = jnp.dot(act_rows, down, preferred_element_type=f32)
        swapped.append(lax.ppermute(mixed[:half_rows].astype(bf16), "expert", swap))
        kept.append(mixed[half_rows:])
    total = resid
    for place, step in enumerate(order):
        pair_sum = (kept[place] + swapped[place].astype(f32)).reshape(n_rows, suffix_len, columns)
        part_sum = pair_sum[0]
        for hop in range(1, n_rows):
            sent = pair_sum[hop].astype(bf16)
            part_sum = part_sum + lax.ppermute(sent, "expert", turn(hop)).astype(f32)
        if step:
            part_sum = lax.ppermute(part_sum.astype(bf16), "donor", rotation(n_donor, step))
        total = total + part_sum.astype(f32)
    return (total.astype(bf16), head_out)


def solution(mesh):
    in_specs = (
        P(("groups", "expert"), None),
        P(("groups", "expert"), "donor"),
        P(("groups", "expert"), None, None),
        P(("groups", "expert", "donor"), None, None, None),
        P("groups", None),
        P("groups"),
        P("donor", "expert"),
        P(),
        P(("groups", "expert"), None),
        P(("groups", "expert"), None),
        P(("expert", "donor"), None, None, None),
        P(("expert", "donor"), None, None),
    )
    out_specs = (P(("groups", "expert"), "donor"), P(("groups", "expert"), "donor"))
    return jax.shard_map(shards, mesh=mesh, in_specs=in_specs, out_specs=out_specs, check_vma=False)
```

```python
import jax
import jax.numpy as jnp
from jax import lax
from jax.sharding import PartitionSpec as P


def rotation(count, step):
    return [(i, (i + step) % count) for i in range(count)]


def pick(array, index, axis=0):
    return lax.dynamic_index_in_dim(array, index, axis, keepdims=False)


def attention(queries, suffix_kv, kv_pool, page_table, prefix_len):
    n_expert = lax.axis_size("expert")
    n_donor = lax.axis_size("donor")
    expert_index = lax.axis_index("expert")
    donor_index = lax.axis_index("donor")
    seq_count, page_count = page_table.shape
    suffix_len = queries.shape[0]
    kv_heads = suffix_kv.shape[1]
    head_dim = suffix_kv.shape[2] // 2
    page_len = kv_pool.shape[2]
    my_group = donor_index * kv_heads // n_donor
    owner_index = expert_index * n_donor + donor_index
    owner_of = page_table // seq_count
    held_slot = jnp.sum(jnp.where(owner_of == owner_index, page_table % seq_count, 0), axis=1)
    dest_group = jnp.arange(n_donor, dtype=jnp.int32) * kv_heads // n_donor
    wanted = (held_slot[:, None] * kv_heads + dest_group[None, :]).reshape(-1)
    outgoing = jnp.take(
        kv_pool.reshape(seq_count * kv_heads, page_len, 2 * head_dim), wanted, axis=0
    )
    arrived = lax.all_to_all(outgoing, ("expert", "donor"), split_axis=0, concat_axis=0, tiled=True)
    my_owners = lax.dynamic_index_in_dim(owner_of, expert_index, 0, keepdims=False)
    ordered = jnp.take(arrived, my_owners, axis=0).reshape(page_count * page_len, 2 * head_dim)
    prefix_keys = ordered[:, :head_dim]
    prefix_vals = ordered[:, head_dim:]
    score_scale = head_dim ** (-0.5)
    query_heads = queries.reshape(suffix_len, -1, head_dim)
    fresh_pair = lax.dynamic_index_in_dim(suffix_kv, my_group, 1, keepdims=False)
    causal = jnp.arange(suffix_len)[:, None] >= jnp.arange(suffix_len)[None, :]
    fresh_scores = (
        jnp.einsum(
            "thc,uc->thu", query_heads, fresh_pair[:, :head_dim], preferred_element_type=jnp.float32
        )
        * score_scale
    )
    fresh_scores = jnp.where(causal[:, None, :], fresh_scores, -jnp.inf)
    prefix_tokens = lax.dynamic_index_in_dim(prefix_len, expert_index, 0, keepdims=False)
    block_keys = min(1024, page_count * page_len)
    live_blocks = (prefix_tokens + block_keys - 1) // block_keys

    def block_scores(block_index):
        keys_block = lax.dynamic_slice_in_dim(prefix_keys, block_index * block_keys, block_keys, 0)
        raw_scores = (
            jnp.einsum("thc,kc->thk", query_heads, keys_block, preferred_element_type=jnp.float32)
            * score_scale
        )
        visible = block_index * block_keys + jnp.arange(block_keys) < prefix_tokens
        return jnp.where(visible[None, None, :], raw_scores, -jnp.inf)

    def raise_max(block_index, running):
        return jnp.maximum(running, jnp.max(block_scores(block_index), axis=2))

    row_max = lax.fori_loop(0, live_blocks, raise_max, jnp.max(fresh_scores, axis=2))

    def add_block(block_index, loop_state):
        row_total, weighted = loop_state
        exp_scores = jnp.exp(block_scores(block_index) - row_max[:, :, None])
        vals_block = lax.dynamic_slice_in_dim(prefix_vals, block_index * block_keys, block_keys, 0)
        weighted = weighted + jnp.einsum(
            "thk,kc->thc",
            exp_scores.astype(jnp.bfloat16),
            vals_block,
            preferred_element_type=jnp.float32,
        )
        return (row_total + jnp.sum(exp_scores, axis=2), weighted)

    fresh_exp = jnp.exp(fresh_scores - row_max[:, :, None])
    start_state = (
        jnp.sum(fresh_exp, axis=2),
        jnp.einsum(
            "thu,uc->thc",
            fresh_exp.astype(jnp.bfloat16),
            fresh_pair[:, head_dim:],
            preferred_element_type=jnp.float32,
        ),
    )
    row_total, weighted = lax.fori_loop(0, live_blocks, add_block, start_state)
    return (weighted / row_total[:, :, None]).astype(jnp.bfloat16).reshape(suffix_len, -1)


def shards(
    hidden_in,
    queries,
    suffix_kv,
    kv_pool,
    page_table,
    prefix_len,
    out_weight,
    norm_gain,
    expert_ids,
    route_probs,
    w_gate_up,
    w_down,
):
    f32, bf16 = jnp.float32, jnp.bfloat16
    n_expert = lax.axis_size("expert")
    n_donor = lax.axis_size("donor")
    expert_index = lax.axis_index("expert")
    z = lax.axis_index("donor")
    n_rows = n_expert // 2
    y = expert_index // 2
    core = expert_index % 2
    swap = [(i, i ^ 1) for i in range(n_expert)]

    def turn(step):
        return rotation(n_expert, 2 * step)

    suffix_len, model_width = hidden_in.shape
    experts_all = 2 * n_expert
    ff_local = w_gate_up.shape[3]
    share_count = n_donor // 2
    my_expert = 2 * expert_index + z // share_count
    pair_cols = model_width // n_rows
    part_rows = n_rows * suffix_len // n_donor
    parts_per_seq = suffix_len // part_rows
    columns = model_width // n_donor
    steps = sorted(range(1, n_donor), key=lambda step: min(step, n_donor - step))

    gates = route_probs / jnp.sum(route_probs, axis=1, keepdims=True)
    hits = expert_ids[:, :, None] == jnp.arange(experts_all, dtype=jnp.int32)
    gate_table = jnp.sum(jnp.where(hits, gates[:, :, None], 0.0), axis=1).T
    tables = [gate_table] + [
        lax.ppermute(gate_table, "expert", rotation(n_expert, step)) for step in range(1, n_expert)
    ]

    other_weight = lax.ppermute(out_weight, "expert", swap)

    part_owner = z * part_rows // suffix_len
    hidden_rows = lax.dynamic_slice_in_dim(hidden_in, z * part_rows % suffix_len, part_rows, 0)

    def hidden_block(row):
        return lax.dynamic_slice_in_dim(hidden_rows, row * pair_cols, pair_cols, 1)

    hidden_part = hidden_block(y)
    for step in range(1, n_rows):
        got = lax.ppermute(hidden_block((y + step) % n_rows), "expert", turn(step))
        hidden_part = jnp.where((y - step) % n_rows == part_owner, got, hidden_part)

    head_out = attention(queries, suffix_kv, kv_pool, page_table, prefix_len)

    heads = jnp.zeros((n_rows, suffix_len, head_out.shape[1]), bf16)
    heads = lax.dynamic_update_index_in_dim(heads, head_out, y, 0)
    for step in range(1, n_rows):
        got = lax.ppermute(head_out, "expert", turn(step))
        got, tables = lax.optimization_barrier((got, tables))
        heads = lax.dynamic_update_index_in_dim(heads, got, (y - step) % n_rows, 0)
    heads = heads.reshape(n_donor, part_rows, -1)
    heads = jnp.concatenate([pick(heads, (z + step) % n_donor) for step in range(n_donor)])
    own_terms = jnp.dot(heads, out_weight, preferred_element_type=f32)
    other_terms = jnp.dot(heads, other_weight, preferred_element_type=f32)

    def term(step):
        rows = slice(step * part_rows, (step + 1) * part_rows)
        own, other = own_terms[rows], other_terms[rows]
        return jnp.concatenate(
            [jnp.where(core == 0, own, other), jnp.where(core == 0, other, own)], axis=1
        )

    own_terms, other_terms, w_gate_up = lax.optimization_barrier(
        (own_terms, other_terms, w_gate_up)
    )
    gate_up_weight = w_gate_up[0].reshape(model_width, 2 * ff_local)
    gots = [
        lax.ppermute(term(step).astype(bf16), "donor", rotation(n_donor, step)) for step in steps
    ]
    gots, gate_up_weight = lax.optimization_barrier((gots, gate_up_weight))
    total = term(0) + hidden_part.astype(f32)
    for got in gots:
        total = total + got.astype(f32)
    chunk = total.astype(bf16)

    all_gates = jnp.stack([pick(table, my_expert) for table in tables], axis=0)

    def core_gates(which):
        rows = [pick(all_gates, (expert_index - 2 * r - which) % n_expert) for r in range(n_rows)]
        return jnp.concatenate(rows).reshape(n_donor, part_rows)

    own_gates, other_gates = core_gates(core), core_gates(1 - core)

    gain_f = norm_gain.astype(f32)
    resid_parts = [None] * n_donor
    own_act, other_act = [None] * n_donor, [None] * n_donor
    batch = max(1, n_donor // 2)
    own_rows, other_rows, row_gates = [], [], []
    for slot in range(n_donor):
        part = (z - slot) % n_donor
        gots = [lax.ppermute(chunk, "expert", turn(hop)) for hop in range(1, n_rows)]
        here = chunk
        if slot < n_donor - 1:
            chunk = lax.ppermute(chunk, "donor", rotation(n_donor, 1))
            chunk, gots = lax.optimization_barrier((chunk, gots))
        if slot == n_donor - 1 and slot >= batch:
            gots, own_act[:batch], other_act[:batch] = lax.optimization_barrier(
                (gots, own_act[:batch], other_act[:batch])
            )
        if n_rows == 2:
            block = jnp.concatenate(
                [jnp.where(y == 0, here, gots[0]), jnp.where(y == 0, gots[0], here)], axis=1
            )
        else:
            block = jnp.zeros((part_rows, n_rows, pair_cols), bf16)
            block = lax.dynamic_update_index_in_dim(block, here, y, 1)
            for hop, got in enumerate(gots, 1):
                block = lax.dynamic_update_index_in_dim(block, got, (y - hop) % n_rows, 1)
            block = block.reshape(part_rows, model_width)
        resid_parts[slot] = lax.dynamic_slice_in_dim(block, z * columns, columns, 1)
        block_f = block.astype(f32)
        inverse = lax.rsqrt(jnp.mean(block_f * block_f, axis=1, keepdims=True) + 1e-06)
        normed = (block_f * inverse * gain_f[None, :]).astype(bf16)
        own_rows.append(normed)
        other_rows.append(lax.ppermute(normed, "expert", swap))
        row_gates.append((pick(own_gates, part), pick(other_gates, part)))
        if len(row_gates) == batch:
            rows_in = jnp.concatenate(own_rows + other_rows, axis=0)
            scale = jnp.concatenate([g[0] for g in row_gates] + [g[1] for g in row_gates])
            gate_up = jnp.dot(rows_in, gate_up_weight, preferred_element_type=f32)
            act = jax.nn.silu(gate_up[:, :ff_local]) * gate_up[:, ff_local:]
            act = (act * scale[:, None]).astype(bf16).reshape(2, batch, part_rows, ff_local)
            for i in range(batch):
                own_act[slot - batch + 1 + i] = act[0, i]
                other_act[slot - batch + 1 + i] = act[1, i]
            own_rows, other_rows, row_gates = [], [], []

    def by_sequence(parts, rows):
        stacked = jnp.stack(parts, axis=0)
        return jnp.concatenate(
            [
                pick(stacked, (z - (y + r) % n_rows * parts_per_seq - i) % n_donor)
                for r in range(rows)
                for i in range(parts_per_seq)
            ],
            axis=0,
        )

    act_rows = jnp.concatenate(
        [by_sequence(other_act, n_rows), by_sequence(own_act, n_rows)], axis=0
    )
    half_rows = n_rows * suffix_len
    resid = by_sequence(resid_parts, 1).astype(f32)

    swapped, kept = [], []
    order = steps[::-1] + [0]
    for place, step in enumerate(order):
        if place >= 2:
            act_rows, swapped[place - 2] = lax.optimization_barrier((act_rows, swapped[place - 2]))
        down = lax.dynamic_slice_in_dim(w_down[0], (z + step) % n_donor * columns, columns, 1)
        mixed = jnp.dot(act_rows, down, preferred_element_type=f32)
        swapped.append(lax.ppermute(mixed[:half_rows].astype(bf16), "expert", swap))
        kept.append(mixed[half_rows:])
    pending = []
    for place in range(n_donor):
        pair_sum = (kept[place] + swapped[place].astype(f32)).reshape(n_rows, suffix_len, columns)
        arriving = [
            lax.ppermute(pair_sum[hop].astype(bf16), "expert", turn(hop)) for hop in range(1, n_rows)
        ]
        pending.append((pair_sum[0], arriving))
    first = pending[0][0]
    first, swapped[-1] = lax.optimization_barrier((first, swapped[-1]))
    total = resid
    for place, step in enumerate(order):
        part_sum, arriving = pending[place]
        if place == 0:
            part_sum = first
        for got in arriving:
            part_sum = part_sum + got.astype(f32)
        if step:
            part_sum = lax.ppermute(part_sum.astype(bf16), "donor", rotation(n_donor, step))
        total = total + part_sum.astype(f32)
    return (total.astype(bf16), head_out)


def solution(mesh):
    in_specs = (
        P(("groups", "expert"), None),
        P(("groups", "expert"), "donor"),
        P(("groups", "expert"), None, None),
        P(("groups", "expert", "donor"), None, None, None),
        P("groups", None),
        P("groups"),
        P("donor", "expert"),
        P(),
        P(("groups", "expert"), None),
        P(("groups", "expert"), None),
        P(("expert", "donor"), None, None, None),
        P(("expert", "donor"), None, None),
    )
    out_specs = (P(("groups", "expert"), "donor"), P(("groups", "expert"), "donor"))
    return jax.shard_map(shards, mesh=mesh, in_specs=in_specs, out_specs=out_specs, check_vma=False)
```

```python
import jax
import jax.numpy as jnp
from jax import lax
from jax.experimental import pallas as pl
from jax.experimental.pallas import tpu as pltpu
from jax.sharding import PartitionSpec as P


def rotation(count, step):
    return [(i, (i + step) % count) for i in range(count)]


def pick(array, index, axis=0):
    return lax.dynamic_index_in_dim(array, index, axis, keepdims=False)


def after(array, *others):
    return lax.optimization_barrier((array, *others))[0]


def hidden_units_kernel(count, *refs):
    rows, (scale_ref, weight_ref, out_ref, total) = refs[:count], refs[count:]
    step = pl.program_id(0)
    block = jnp.concatenate([ref[...] for ref in rows], axis=0)
    part = jnp.dot(block, weight_ref[...], preferred_element_type=jnp.float32)

    @pl.when(step == 0)
    def _():
        total[...] = part

    @pl.when(step > 0)
    def _():
        total[...] += part

    @pl.when(step == pl.num_programs(0) - 1)
    def _():
        units = out_ref.shape[1]
        gate, up = total[:, :units], total[:, units:]
        act = gate / (1.0 + jnp.exp(-gate)) * up
        out_ref[...] = (act * scale_ref[...]).astype(out_ref.dtype)


def hidden_units(rows, scale, weight):
    model_width, units = weight.shape
    height = sum(part.shape[0] for part in rows)
    depth = min(512, model_width)
    row_specs = [pl.BlockSpec((part.shape[0], depth), lambda k: (0, k)) for part in rows]
    return pl.pallas_call(
        lambda *refs: hidden_units_kernel(len(rows), *refs),
        grid=(model_width // depth,),
        in_specs=row_specs
        + [
            pl.BlockSpec((height, 1), lambda k: (0, 0)),
            pl.BlockSpec((depth, units), lambda k: (k, 0)),
        ],
        out_specs=pl.BlockSpec((height, units // 2), lambda k: (0, 0)),
        out_shape=jax.ShapeDtypeStruct((height, units // 2), jnp.bfloat16),
        scratch_shapes=[pltpu.VMEM((height, units), jnp.float32)],
        compiler_params=pltpu.CompilerParams(vmem_limit_bytes=24 * 1024 * 1024),
    )(*rows, scale, weight)


def attention(queries, suffix_kv, kv_pool, page_table, prefix_len):
    n_expert = lax.axis_size("expert")
    n_donor = lax.axis_size("donor")
    expert_index = lax.axis_index("expert")
    donor_index = lax.axis_index("donor")
    seq_count, page_count = page_table.shape
    suffix_len = queries.shape[0]
    kv_heads = suffix_kv.shape[1]
    head_dim = suffix_kv.shape[2] // 2
    page_len = kv_pool.shape[2]
    my_group = donor_index * kv_heads // n_donor
    owner_index = expert_index * n_donor + donor_index
    owner_of = page_table // seq_count
    held_slot = jnp.sum(jnp.where(owner_of == owner_index, page_table % seq_count, 0), axis=1)
    dest_group = jnp.arange(n_donor, dtype=jnp.int32) * kv_heads // n_donor
    wanted = (held_slot[:, None] * kv_heads + dest_group[None, :]).reshape(-1)
    outgoing = jnp.take(
        kv_pool.reshape(seq_count * kv_heads, page_len, 2 * head_dim), wanted, axis=0
    )
    arrived = lax.all_to_all(outgoing, ("expert", "donor"), split_axis=0, concat_axis=0, tiled=True)
    my_owners = lax.dynamic_index_in_dim(owner_of, expert_index, 0, keepdims=False)
    ordered = jnp.take(arrived, my_owners, axis=0).reshape(page_count * page_len, 2 * head_dim)
    prefix_keys = ordered[:, :head_dim]
    prefix_vals = ordered[:, head_dim:]
    score_scale = head_dim ** (-0.5)
    query_heads = queries.reshape(suffix_len, -1, head_dim)
    fresh_pair = lax.dynamic_index_in_dim(suffix_kv, my_group, 1, keepdims=False)
    causal = jnp.arange(suffix_len)[:, None] >= jnp.arange(suffix_len)[None, :]
    fresh_scores = (
        jnp.einsum(
            "thc,uc->thu", query_heads, fresh_pair[:, :head_dim], preferred_element_type=jnp.float32
        )
        * score_scale
    )
    fresh_scores = jnp.where(causal[:, None, :], fresh_scores, -jnp.inf)
    prefix_tokens = lax.dynamic_index_in_dim(prefix_len, expert_index, 0, keepdims=False)
    block_keys = min(1024, page_count * page_len)
    live_blocks = (prefix_tokens + block_keys - 1) // block_keys

    def block_scores(block_index):
        keys_block = lax.dynamic_slice_in_dim(prefix_keys, block_index * block_keys, block_keys, 0)
        raw_scores = (
            jnp.einsum("thc,kc->thk", query_heads, keys_block, preferred_element_type=jnp.float32)
            * score_scale
        )
        visible = block_index * block_keys + jnp.arange(block_keys) < prefix_tokens
        return jnp.where(visible[None, None, :], raw_scores, -jnp.inf)

    def raise_max(block_index, running):
        return jnp.maximum(running, jnp.max(block_scores(block_index), axis=2))

    row_max = lax.fori_loop(0, live_blocks, raise_max, jnp.max(fresh_scores, axis=2))

    def add_block(block_index, loop_state):
        row_total, weighted = loop_state
        exp_scores = jnp.exp(block_scores(block_index) - row_max[:, :, None])
        vals_block = lax.dynamic_slice_in_dim(prefix_vals, block_index * block_keys, block_keys, 0)
        weighted = weighted + jnp.einsum(
            "thk,kc->thc",
            exp_scores.astype(jnp.bfloat16),
            vals_block,
            preferred_element_type=jnp.float32,
        )
        return (row_total + jnp.sum(exp_scores, axis=2), weighted)

    fresh_exp = jnp.exp(fresh_scores - row_max[:, :, None])
    start_state = (
        jnp.sum(fresh_exp, axis=2),
        jnp.einsum(
            "thu,uc->thc",
            fresh_exp.astype(jnp.bfloat16),
            fresh_pair[:, head_dim:],
            preferred_element_type=jnp.float32,
        ),
    )
    row_total, weighted = lax.fori_loop(0, live_blocks, add_block, start_state)
    return (weighted / row_total[:, :, None]).astype(jnp.bfloat16).reshape(suffix_len, -1)


def shards(
    hidden_in,
    queries,
    suffix_kv,
    kv_pool,
    page_table,
    prefix_len,
    out_weight,
    norm_gain,
    expert_ids,
    route_probs,
    w_gate_up,
    w_down,
):
    f32, bf16 = jnp.float32, jnp.bfloat16
    n_expert = lax.axis_size("expert")
    n_donor = lax.axis_size("donor")
    expert_index = lax.axis_index("expert")
    z = lax.axis_index("donor")
    n_rows = n_expert // 2
    y = expert_index // 2
    core = expert_index % 2
    swap = [(i, i ^ 1) for i in range(n_expert)]

    def turn(step):
        return rotation(n_expert, 2 * step)

    suffix_len, model_width = hidden_in.shape
    experts_all = 2 * n_expert
    ff_local = w_gate_up.shape[3]
    share_count = n_donor // 2
    my_expert = 2 * expert_index + z // share_count
    pair_cols = model_width // n_rows
    part_rows = n_rows * suffix_len // n_donor
    parts_per_seq = suffix_len // part_rows
    columns = model_width // n_donor
    steps = sorted(range(1, n_donor), key=lambda step: min(step, n_donor - step))

    gates = route_probs / jnp.sum(route_probs, axis=1, keepdims=True)
    hits = expert_ids[:, :, None] == jnp.arange(experts_all, dtype=jnp.int32)
    gate_table = jnp.sum(jnp.where(hits, gates[:, :, None], 0.0), axis=1).T
    tables = [gate_table] + [
        lax.ppermute(gate_table, "expert", rotation(n_expert, step)) for step in range(1, n_expert)
    ]

    other_weight = lax.ppermute(out_weight, "expert", swap)

    part_owner = z * part_rows // suffix_len
    hidden_rows = lax.dynamic_slice_in_dim(hidden_in, z * part_rows % suffix_len, part_rows, 0)

    def hidden_block(row):
        return lax.dynamic_slice_in_dim(hidden_rows, row * pair_cols, pair_cols, 1)

    hidden_part = hidden_block(y)
    for step in range(1, n_rows):
        got = lax.ppermute(hidden_block((y + step) % n_rows), "expert", turn(step))
        hidden_part = jnp.where((y - step) % n_rows == part_owner, got, hidden_part)

    head_out = attention(queries, suffix_kv, kv_pool, page_table, prefix_len)

    heads = jnp.zeros((n_rows, suffix_len, head_out.shape[1]), bf16)
    heads = lax.dynamic_update_index_in_dim(heads, head_out, y, 0)
    for step in range(1, n_rows):
        got = lax.ppermute(head_out, "expert", turn(step))
        got, tables = lax.optimization_barrier((got, tables))
        heads = lax.dynamic_update_index_in_dim(heads, got, (y - step) % n_rows, 0)
    heads = heads.reshape(n_donor, part_rows, -1)
    heads = jnp.concatenate([pick(heads, (z + step) % n_donor) for step in range(n_donor)])
    own_terms = jnp.dot(heads, out_weight, preferred_element_type=f32)
    other_terms = jnp.dot(heads, other_weight, preferred_element_type=f32)

    def term(step):
        rows = slice(step * part_rows, (step + 1) * part_rows)
        own, other = own_terms[rows], other_terms[rows]
        return jnp.concatenate(
            [jnp.where(core == 0, own, other), jnp.where(core == 0, other, own)], axis=1
        )

    own_terms, other_terms, w_gate_up = lax.optimization_barrier(
        (own_terms, other_terms, w_gate_up)
    )
    gate_up_weight = w_gate_up[0].reshape(model_width, 2 * ff_local)
    gots = [
        lax.ppermute(term(step).astype(bf16), "donor", rotation(n_donor, step)) for step in steps
    ]
    gots, gate_up_weight = lax.optimization_barrier((gots, gate_up_weight))
    total = term(0) + hidden_part.astype(f32)
    for got in gots:
        total = total + got.astype(f32)
    chunk = total.astype(bf16)

    all_gates = jnp.stack([pick(table, my_expert) for table in tables], axis=0)

    def core_gates(which):
        rows = [pick(all_gates, (expert_index - 2 * r - which) % n_expert) for r in range(n_rows)]
        return jnp.concatenate(rows).reshape(n_donor, part_rows)

    own_gates, other_gates = core_gates(core), core_gates(1 - core)

    gain_f = norm_gain.astype(f32)
    resid_parts = [None] * n_donor
    own_act, other_act = [None] * n_donor, [None] * n_donor
    batch = max(1, n_donor // 2)
    own_rows, other_rows, row_gates = [], [], []
    for slot in range(n_donor):
        part = (z - slot) % n_donor
        gots = [lax.ppermute(chunk, "expert", turn(hop)) for hop in range(1, n_rows)]
        here = chunk
        if slot < n_donor - 1:
            chunk = lax.ppermute(chunk, "donor", rotation(n_donor, 1))
            chunk, gots = lax.optimization_barrier((chunk, gots))
        if slot == n_donor - 1 and slot >= batch:
            gots, own_act[:batch], other_act[:batch] = lax.optimization_barrier(
                (gots, own_act[:batch], other_act[:batch])
            )
        if n_rows == 2:
            block = jnp.concatenate(
                [jnp.where(y == 0, here, gots[0]), jnp.where(y == 0, gots[0], here)], axis=1
            )
        else:
            block = jnp.zeros((part_rows, n_rows, pair_cols), bf16)
            block = lax.dynamic_update_index_in_dim(block, here, y, 1)
            for hop, got in enumerate(gots, 1):
                block = lax.dynamic_update_index_in_dim(block, got, (y - hop) % n_rows, 1)
            block = block.reshape(part_rows, model_width)
        resid_parts[slot] = lax.dynamic_slice_in_dim(block, z * columns, columns, 1)
        block_f = block.astype(f32)
        inverse = lax.rsqrt(jnp.mean(block_f * block_f, axis=1, keepdims=True) + 1e-06)
        normed = (block_f * inverse * gain_f[None, :]).astype(bf16)
        own_rows.append(normed)
        other_rows.append(lax.ppermute(normed, "expert", swap))
        row_gates.append((pick(own_gates, part), pick(other_gates, part)))
        if len(row_gates) == batch:
            scale = jnp.concatenate([g[0] for g in row_gates] + [g[1] for g in row_gates])
            act = hidden_units(own_rows + other_rows, scale[:, None], gate_up_weight)
            act = act.reshape(2, batch, part_rows, ff_local)
            for i in range(batch):
                own_act[slot - batch + 1 + i] = act[0, i]
                other_act[slot - batch + 1 + i] = act[1, i]
            own_rows, other_rows, row_gates = [], [], []

    def by_sequence(parts, rows):
        stacked = jnp.stack(parts, axis=0)
        return jnp.concatenate(
            [
                pick(stacked, (z - (y + r) % n_rows * parts_per_seq - i) % n_donor)
                for r in range(rows)
                for i in range(parts_per_seq)
            ],
            axis=0,
        )

    act_rows = jnp.concatenate(
        [by_sequence(other_act, n_rows), by_sequence(own_act, n_rows)], axis=0
    )
    half_rows = n_rows * suffix_len
    resid = by_sequence(resid_parts, 1).astype(f32)

    swapped, kept = [], []
    order = steps[::-1] + [0]
    for place, step in enumerate(order):
        if place >= 2:
            act_rows, swapped[place - 2] = lax.optimization_barrier((act_rows, swapped[place - 2]))
        down = lax.dynamic_slice_in_dim(w_down[0], (z + step) % n_donor * columns, columns, 1)
        mixed = jnp.dot(act_rows, down, preferred_element_type=f32)
        swapped.append(lax.ppermute(mixed[:half_rows].astype(bf16), "expert", swap))
        kept.append(mixed[half_rows:])
    pending = []
    for place in range(n_donor):
        pair_sum = (kept[place] + swapped[place].astype(f32)).reshape(n_rows, suffix_len, columns)
        arriving = [
            lax.ppermute(pair_sum[hop].astype(bf16), "expert", turn(hop)) for hop in range(1, n_rows)
        ]
        pending.append((pair_sum[0], arriving))
    total, before = resid, swapped[-2:]
    for place, step in enumerate(order):
        part_sum, arriving = pending[place]
        part_sum = after(part_sum, *before)
        for got in arriving:
            part_sum = part_sum + got.astype(f32)
        before = [part_sum]
        if step:
            part_sum = lax.ppermute(part_sum.astype(bf16), "donor", rotation(n_donor, step))
        total = total + part_sum.astype(f32)
    return (total.astype(bf16), head_out)


def solution(mesh):
    in_specs = (
        P(("groups", "expert"), None),
        P(("groups", "expert"), "donor"),
        P(("groups", "expert"), None, None),
        P(("groups", "expert", "donor"), None, None, None),
        P("groups", None),
        P("groups"),
        P("donor", "expert"),
        P(),
        P(("groups", "expert"), None),
        P(("groups", "expert"), None),
        P(("expert", "donor"), None, None, None),
        P(("expert", "donor"), None, None),
    )
    out_specs = (P(("groups", "expert"), "donor"), P(("groups", "expert"), "donor"))
    return jax.shard_map(shards, mesh=mesh, in_specs=in_specs, out_specs=out_specs, check_vma=False)
```

```python
import jax
import jax.numpy as jnp
from jax import lax
from jax.experimental import pallas as pl
from jax.experimental.pallas import tpu as pltpu
from jax.sharding import PartitionSpec as P


def rotation(count, step):
    return [(i, (i + step) % count) for i in range(count)]


def pick(array, index, axis=0):
    return lax.dynamic_index_in_dim(array, index, axis, keepdims=False)


def after(array, *others):
    return lax.optimization_barrier((array, *others))[0]


def bring_kernel(source, target, sem):
    copy = pltpu.make_async_copy(source, target, sem)
    copy.start()
    copy.wait()


def bring(array):
    return pl.pallas_call(
        bring_kernel,
        in_specs=[pl.BlockSpec(memory_space=pl.ANY)],
        out_specs=pl.BlockSpec(memory_space=pltpu.VMEM),
        out_shape=pltpu.VMEM(array.shape, array.dtype),
        scratch_shapes=[pltpu.SemaphoreType.DMA],
        compiler_params=pltpu.CompilerParams(vmem_limit_bytes=1024 * 1024),
    )(array)


def attention(queries, suffix_kv, kv_pool, page_table, prefix_len):
    n_expert = lax.axis_size("expert")
    n_donor = lax.axis_size("donor")
    expert_index = lax.axis_index("expert")
    donor_index = lax.axis_index("donor")
    seq_count, page_count = page_table.shape
    suffix_len = queries.shape[0]
    kv_heads = suffix_kv.shape[1]
    head_dim = suffix_kv.shape[2] // 2
    page_len = kv_pool.shape[2]
    my_group = donor_index * kv_heads // n_donor
    owner_index = expert_index * n_donor + donor_index
    owner_of = page_table // seq_count
    held_slot = jnp.sum(jnp.where(owner_of == owner_index, page_table % seq_count, 0), axis=1)
    dest_group = jnp.arange(n_donor, dtype=jnp.int32) * kv_heads // n_donor
    wanted = (held_slot[:, None] * kv_heads + dest_group[None, :]).reshape(-1)
    outgoing = jnp.take(
        kv_pool.reshape(seq_count * kv_heads, page_len, 2 * head_dim), wanted, axis=0
    )
    arrived = lax.all_to_all(outgoing, ("expert", "donor"), split_axis=0, concat_axis=0, tiled=True)
    my_owners = lax.dynamic_index_in_dim(owner_of, expert_index, 0, keepdims=False)
    ordered = jnp.take(arrived, my_owners, axis=0).reshape(page_count * page_len, 2 * head_dim)
    prefix_keys = ordered[:, :head_dim]
    prefix_vals = ordered[:, head_dim:]
    score_scale = head_dim ** (-0.5)
    query_heads = queries.reshape(suffix_len, -1, head_dim)
    fresh_pair = lax.dynamic_index_in_dim(suffix_kv, my_group, 1, keepdims=False)
    causal = jnp.arange(suffix_len)[:, None] >= jnp.arange(suffix_len)[None, :]
    fresh_scores = (
        jnp.einsum(
            "thc,uc->thu", query_heads, fresh_pair[:, :head_dim], preferred_element_type=jnp.float32
        )
        * score_scale
    )
    fresh_scores = jnp.where(causal[:, None, :], fresh_scores, -jnp.inf)
    prefix_tokens = lax.dynamic_index_in_dim(prefix_len, expert_index, 0, keepdims=False)
    block_keys = min(1024, page_count * page_len)
    live_blocks = (prefix_tokens + block_keys - 1) // block_keys

    def block_scores(block_index):
        keys_block = lax.dynamic_slice_in_dim(prefix_keys, block_index * block_keys, block_keys, 0)
        raw_scores = (
            jnp.einsum("thc,kc->thk", query_heads, keys_block, preferred_element_type=jnp.float32)
            * score_scale
        )
        visible = block_index * block_keys + jnp.arange(block_keys) < prefix_tokens
        return jnp.where(visible[None, None, :], raw_scores, -jnp.inf)

    def raise_max(block_index, running):
        return jnp.maximum(running, jnp.max(block_scores(block_index), axis=2))

    row_max = lax.fori_loop(0, live_blocks, raise_max, jnp.max(fresh_scores, axis=2))

    def add_block(block_index, loop_state):
        row_total, weighted = loop_state
        exp_scores = jnp.exp(block_scores(block_index) - row_max[:, :, None])
        vals_block = lax.dynamic_slice_in_dim(prefix_vals, block_index * block_keys, block_keys, 0)
        weighted = weighted + jnp.einsum(
            "thk,kc->thc",
            exp_scores.astype(jnp.bfloat16),
            vals_block,
            preferred_element_type=jnp.float32,
        )
        return (row_total + jnp.sum(exp_scores, axis=2), weighted)

    fresh_exp = jnp.exp(fresh_scores - row_max[:, :, None])
    start_state = (
        jnp.sum(fresh_exp, axis=2),
        jnp.einsum(
            "thu,uc->thc",
            fresh_exp.astype(jnp.bfloat16),
            fresh_pair[:, head_dim:],
            preferred_element_type=jnp.float32,
        ),
    )
    row_total, weighted = lax.fori_loop(0, live_blocks, add_block, start_state)
    return (weighted / row_total[:, :, None]).astype(jnp.bfloat16).reshape(suffix_len, -1)


def shards(
    hidden_in,
    queries,
    suffix_kv,
    kv_pool,
    page_table,
    prefix_len,
    out_weight,
    norm_gain,
    expert_ids,
    route_probs,
    w_gate_up,
    w_down,
):
    f32, bf16 = jnp.float32, jnp.bfloat16
    n_expert = lax.axis_size("expert")
    n_donor = lax.axis_size("donor")
    expert_index = lax.axis_index("expert")
    z = lax.axis_index("donor")
    n_rows = n_expert // 2
    y = expert_index // 2
    core = expert_index % 2
    swap = [(i, i ^ 1) for i in range(n_expert)]

    def turn(step):
        return rotation(n_expert, 2 * step)

    suffix_len, model_width = hidden_in.shape
    experts_all = 2 * n_expert
    ff_local = w_gate_up.shape[3]
    share_count = n_donor // 2
    my_expert = 2 * expert_index + z // share_count
    pair_cols = model_width // n_rows
    part_rows = n_rows * suffix_len // n_donor
    parts_per_seq = suffix_len // part_rows
    columns = model_width // n_donor
    steps = sorted(range(1, n_donor), key=lambda step: min(step, n_donor - step))

    gates = route_probs / jnp.sum(route_probs, axis=1, keepdims=True)
    hits = expert_ids[:, :, None] == jnp.arange(experts_all, dtype=jnp.int32)
    gate_table = jnp.sum(jnp.where(hits, gates[:, :, None], 0.0), axis=1).T
    tables = [gate_table] + [
        lax.ppermute(gate_table, "expert", rotation(n_expert, step)) for step in range(1, n_expert)
    ]

    other_weight = lax.ppermute(out_weight, "expert", swap)

    part_owner = z * part_rows // suffix_len
    hidden_rows = lax.dynamic_slice_in_dim(hidden_in, z * part_rows % suffix_len, part_rows, 0)

    def hidden_block(row):
        return lax.dynamic_slice_in_dim(hidden_rows, row * pair_cols, pair_cols, 1)

    hidden_part = hidden_block(y)
    for step in range(1, n_rows):
        got = lax.ppermute(hidden_block((y + step) % n_rows), "expert", turn(step))
        hidden_part = jnp.where((y - step) % n_rows == part_owner, got, hidden_part)

    head_out = attention(queries, suffix_kv, kv_pool, page_table, prefix_len)

    heads = jnp.zeros((n_rows, suffix_len, head_out.shape[1]), bf16)
    heads = lax.dynamic_update_index_in_dim(heads, head_out, y, 0)
    for step in range(1, n_rows):
        got = lax.ppermute(head_out, "expert", turn(step))
        got, tables = lax.optimization_barrier((got, tables))
        heads = lax.dynamic_update_index_in_dim(heads, got, (y - step) % n_rows, 0)
    heads = heads.reshape(n_donor, part_rows, -1)
    heads = jnp.concatenate([pick(heads, (z + step) % n_donor) for step in range(n_donor)])
    own_terms = jnp.dot(heads, out_weight, preferred_element_type=f32)
    other_terms = jnp.dot(heads, other_weight, preferred_element_type=f32)

    def term(step):
        rows = slice(step * part_rows, (step + 1) * part_rows)
        own, other = own_terms[rows], other_terms[rows]
        return jnp.concatenate(
            [jnp.where(core == 0, own, other), jnp.where(core == 0, other, own)], axis=1
        )

    own_terms, other_terms, w_gate_up = lax.optimization_barrier(
        (own_terms, other_terms, w_gate_up)
    )
    gate_up_weight = bring(w_gate_up[0].reshape(model_width, 2 * ff_local))
    gots = [
        lax.ppermute(term(step).astype(bf16), "donor", rotation(n_donor, step)) for step in steps
    ]
    gots, gate_up_weight = lax.optimization_barrier((gots, gate_up_weight))
    total = term(0) + hidden_part.astype(f32)
    for got in gots:
        total = total + got.astype(f32)
    chunk = total.astype(bf16)

    all_gates = jnp.stack([pick(table, my_expert) for table in tables], axis=0)

    def core_gates(which):
        rows = [pick(all_gates, (expert_index - 2 * r - which) % n_expert) for r in range(n_rows)]
        return jnp.concatenate(rows).reshape(n_donor, part_rows)

    own_gates, other_gates = core_gates(core), core_gates(1 - core)

    gain_f = norm_gain.astype(f32)
    resid_parts = [None] * n_donor
    own_act, other_act = [None] * n_donor, [None] * n_donor
    batch = max(1, n_donor // 2)
    own_rows, other_rows, row_gates = [], [], []
    for slot in range(n_donor):
        part = (z - slot) % n_donor
        gots = [lax.ppermute(chunk, "expert", turn(hop)) for hop in range(1, n_rows)]
        here = chunk
        if slot < n_donor - 1:
            chunk = lax.ppermute(chunk, "donor", rotation(n_donor, 1))
            chunk, gots = lax.optimization_barrier((chunk, gots))
        if slot == n_donor - 1 and slot >= batch:
            gots, own_act[:batch], other_act[:batch] = lax.optimization_barrier(
                (gots, own_act[:batch], other_act[:batch])
            )
        if n_rows == 2:
            block = jnp.concatenate(
                [jnp.where(y == 0, here, gots[0]), jnp.where(y == 0, gots[0], here)], axis=1
            )
        else:
            block = jnp.zeros((part_rows, n_rows, pair_cols), bf16)
            block = lax.dynamic_update_index_in_dim(block, here, y, 1)
            for hop, got in enumerate(gots, 1):
                block = lax.dynamic_update_index_in_dim(block, got, (y - hop) % n_rows, 1)
            block = block.reshape(part_rows, model_width)
        resid_parts[slot] = lax.dynamic_slice_in_dim(block, z * columns, columns, 1)
        block_f = block.astype(f32)
        inverse = lax.rsqrt(jnp.mean(block_f * block_f, axis=1, keepdims=True) + 1e-06)
        normed = (block_f * inverse * gain_f[None, :]).astype(bf16)
        own_rows.append(normed)
        other_rows.append(lax.ppermute(normed, "expert", swap))
        row_gates.append((pick(own_gates, part), pick(other_gates, part)))
        if len(row_gates) == batch:
            rows_in = jnp.concatenate(own_rows + other_rows, axis=0)
            scale = jnp.concatenate([g[0] for g in row_gates] + [g[1] for g in row_gates])
            gate_up = jnp.dot(rows_in, gate_up_weight, preferred_element_type=f32)
            act = jax.nn.silu(gate_up[:, :ff_local]) * gate_up[:, ff_local:]
            act = (act * scale[:, None]).astype(bf16).reshape(2, batch, part_rows, ff_local)
            for i in range(batch):
                own_act[slot - batch + 1 + i] = act[0, i]
                other_act[slot - batch + 1 + i] = act[1, i]
            own_rows, other_rows, row_gates = [], [], []

    def by_sequence(parts, rows):
        stacked = jnp.stack(parts, axis=0)
        return jnp.concatenate(
            [
                pick(stacked, (z - (y + r) % n_rows * parts_per_seq - i) % n_donor)
                for r in range(rows)
                for i in range(parts_per_seq)
            ],
            axis=0,
        )

    act_rows = jnp.concatenate(
        [by_sequence(other_act, n_rows), by_sequence(own_act, n_rows)], axis=0
    )
    half_rows = n_rows * suffix_len
    resid = by_sequence(resid_parts, 1).astype(f32)

    swapped, kept = [], []
    order = steps[::-1] + [0]
    for place, step in enumerate(order):
        if place >= 2:
            act_rows, swapped[place - 2] = lax.optimization_barrier((act_rows, swapped[place - 2]))
        down = lax.dynamic_slice_in_dim(w_down[0], (z + step) % n_donor * columns, columns, 1)
        mixed = jnp.dot(act_rows, down, preferred_element_type=f32)
        swapped.append(lax.ppermute(mixed[:half_rows].astype(bf16), "expert", swap))
        kept.append(mixed[half_rows:])
    pending, before = [], []
    for place in range(n_donor):
        block = kept[place] + after(swapped[place], *before).astype(f32)
        before = [block]
        block = block.reshape(n_rows, suffix_len, columns)
        arriving = [
            lax.ppermute(block[hop].astype(bf16), "expert", turn(hop)) for hop in range(1, n_rows)
        ]
        pending.append((block[0], arriving))
    total = resid
    for place, step in enumerate(order):
        part_sum, arriving = pending[place]
        part_sum = after(part_sum, *before)
        for got in arriving:
            part_sum = part_sum + got.astype(f32)
        before = [part_sum]
        if step:
            part_sum = lax.ppermute(part_sum.astype(bf16), "donor", rotation(n_donor, step))
        total = total + part_sum.astype(f32)
    return (total.astype(bf16), head_out)


def solution(mesh):
    in_specs = (
        P(("groups", "expert"), None),
        P(("groups", "expert"), "donor"),
        P(("groups", "expert"), None, None),
        P(("groups", "expert", "donor"), None, None, None),
        P("groups", None),
        P("groups"),
        P("donor", "expert"),
        P(),
        P(("groups", "expert"), None),
        P(("groups", "expert"), None),
        P(("expert", "donor"), None, None, None),
        P(("expert", "donor"), None, None),
    )
    out_specs = (P(("groups", "expert"), "donor"), P(("groups", "expert"), "donor"))
    return jax.shard_map(shards, mesh=mesh, in_specs=in_specs, out_specs=out_specs, check_vma=False)
```

```python
import jax
import jax.numpy as jnp
from jax import lax
from jax.sharding import PartitionSpec as P


def rotation(count, step):
    return [(i, (i + step) % count) for i in range(count)]


def pick(array, index, axis=0):
    return lax.dynamic_index_in_dim(array, index, axis, keepdims=False)


def after(array, *others):
    return lax.optimization_barrier((array, *others))[0]


def attention(queries, suffix_kv, kv_pool, page_table, prefix_len):
    n_expert = lax.axis_size("expert")
    n_donor = lax.axis_size("donor")
    expert_index = lax.axis_index("expert")
    donor_index = lax.axis_index("donor")
    seq_count, page_count = page_table.shape
    suffix_len = queries.shape[0]
    kv_heads = suffix_kv.shape[1]
    head_dim = suffix_kv.shape[2] // 2
    page_len = kv_pool.shape[2]
    my_group = donor_index * kv_heads // n_donor
    owner_index = expert_index * n_donor + donor_index
    owner_of = page_table // seq_count
    held_slot = jnp.sum(jnp.where(owner_of == owner_index, page_table % seq_count, 0), axis=1)
    dest_group = jnp.arange(n_donor, dtype=jnp.int32) * kv_heads // n_donor
    wanted = (held_slot[:, None] * kv_heads + dest_group[None, :]).reshape(-1)
    outgoing = jnp.take(
        kv_pool.reshape(seq_count * kv_heads, page_len, 2 * head_dim), wanted, axis=0
    )
    arrived = lax.all_to_all(outgoing, ("expert", "donor"), split_axis=0, concat_axis=0, tiled=True)
    my_owners = lax.dynamic_index_in_dim(owner_of, expert_index, 0, keepdims=False)
    ordered = jnp.take(arrived, my_owners, axis=0).reshape(page_count * page_len, 2 * head_dim)
    prefix_keys = ordered[:, :head_dim]
    prefix_vals = ordered[:, head_dim:]
    score_scale = head_dim ** (-0.5)
    query_heads = queries.reshape(suffix_len, -1, head_dim)
    fresh_pair = lax.dynamic_index_in_dim(suffix_kv, my_group, 1, keepdims=False)
    causal = jnp.arange(suffix_len)[:, None] >= jnp.arange(suffix_len)[None, :]
    fresh_scores = (
        jnp.einsum(
            "thc,uc->thu", query_heads, fresh_pair[:, :head_dim], preferred_element_type=jnp.float32
        )
        * score_scale
    )
    fresh_scores = jnp.where(causal[:, None, :], fresh_scores, -jnp.inf)
    prefix_tokens = lax.dynamic_index_in_dim(prefix_len, expert_index, 0, keepdims=False)
    block_keys = min(1024, page_count * page_len)
    live_blocks = (prefix_tokens + block_keys - 1) // block_keys

    def block_scores(block_index):
        keys_block = lax.dynamic_slice_in_dim(prefix_keys, block_index * block_keys, block_keys, 0)
        raw_scores = (
            jnp.einsum("thc,kc->thk", query_heads, keys_block, preferred_element_type=jnp.float32)
            * score_scale
        )
        visible = block_index * block_keys + jnp.arange(block_keys) < prefix_tokens
        return jnp.where(visible[None, None, :], raw_scores, -jnp.inf)

    def raise_max(block_index, running):
        return jnp.maximum(running, jnp.max(block_scores(block_index), axis=2))

    row_max = lax.fori_loop(0, live_blocks, raise_max, jnp.max(fresh_scores, axis=2))

    def add_block(block_index, loop_state):
        row_total, weighted = loop_state
        exp_scores = jnp.exp(block_scores(block_index) - row_max[:, :, None])
        vals_block = lax.dynamic_slice_in_dim(prefix_vals, block_index * block_keys, block_keys, 0)
        weighted = weighted + jnp.einsum(
            "thk,kc->thc",
            exp_scores.astype(jnp.bfloat16),
            vals_block,
            preferred_element_type=jnp.float32,
        )
        return (row_total + jnp.sum(exp_scores, axis=2), weighted)

    fresh_exp = jnp.exp(fresh_scores - row_max[:, :, None])
    start_state = (
        jnp.sum(fresh_exp, axis=2),
        jnp.einsum(
            "thu,uc->thc",
            fresh_exp.astype(jnp.bfloat16),
            fresh_pair[:, head_dim:],
            preferred_element_type=jnp.float32,
        ),
    )
    row_total, weighted = lax.fori_loop(0, live_blocks, add_block, start_state)
    return (weighted / row_total[:, :, None]).astype(jnp.bfloat16).reshape(suffix_len, -1)


def shards(
    hidden_in,
    queries,
    suffix_kv,
    kv_pool,
    page_table,
    prefix_len,
    out_weight,
    norm_gain,
    expert_ids,
    route_probs,
    w_gate_up,
    w_down,
):
    f32, bf16 = jnp.float32, jnp.bfloat16
    n_expert = lax.axis_size("expert")
    n_donor = lax.axis_size("donor")
    expert_index = lax.axis_index("expert")
    z = lax.axis_index("donor")
    n_rows = n_expert // 2
    y = expert_index // 2
    core = expert_index % 2
    swap = [(i, i ^ 1) for i in range(n_expert)]

    def turn(step):
        return rotation(n_expert, 2 * step)

    suffix_len, model_width = hidden_in.shape
    experts_all = 2 * n_expert
    ff_local = w_gate_up.shape[3]
    share_count = n_donor // 2
    my_expert = 2 * expert_index + z // share_count
    pair_cols = model_width // n_rows
    part_rows = n_rows * suffix_len // n_donor
    parts_per_seq = suffix_len // part_rows
    columns = model_width // n_donor
    steps = sorted(range(1, n_donor), key=lambda step: min(step, n_donor - step))

    gates = route_probs / jnp.sum(route_probs, axis=1, keepdims=True)
    hits = expert_ids[:, :, None] == jnp.arange(experts_all, dtype=jnp.int32)
    gate_table = jnp.sum(jnp.where(hits, gates[:, :, None], 0.0), axis=1).T
    tables = [gate_table] + [
        lax.ppermute(gate_table, "expert", rotation(n_expert, step)) for step in range(1, n_expert)
    ]

    other_weight = lax.ppermute(out_weight, "expert", swap)

    part_owner = z * part_rows // suffix_len
    hidden_rows = lax.dynamic_slice_in_dim(hidden_in, z * part_rows % suffix_len, part_rows, 0)

    def hidden_block(row):
        return lax.dynamic_slice_in_dim(hidden_rows, row * pair_cols, pair_cols, 1)

    hidden_part = hidden_block(y)
    for step in range(1, n_rows):
        got = lax.ppermute(hidden_block((y + step) % n_rows), "expert", turn(step))
        hidden_part = jnp.where((y - step) % n_rows == part_owner, got, hidden_part)

    head_out = attention(queries, suffix_kv, kv_pool, page_table, prefix_len)

    heads = jnp.zeros((n_rows, suffix_len, head_out.shape[1]), bf16)
    heads = lax.dynamic_update_index_in_dim(heads, head_out, y, 0)
    for step in range(1, n_rows):
        got = lax.ppermute(head_out, "expert", turn(step))
        got, tables = lax.optimization_barrier((got, tables))
        heads = lax.dynamic_update_index_in_dim(heads, got, (y - step) % n_rows, 0)
    heads = heads.reshape(n_donor, part_rows, -1)
    heads = jnp.concatenate([pick(heads, (z + step) % n_donor) for step in range(n_donor)])
    own_terms = jnp.dot(heads, out_weight, preferred_element_type=f32)
    other_terms = jnp.dot(heads, other_weight, preferred_element_type=f32)

    def term(step):
        rows = slice(step * part_rows, (step + 1) * part_rows)
        own, other = own_terms[rows], other_terms[rows]
        return jnp.concatenate(
            [jnp.where(core == 0, own, other), jnp.where(core == 0, other, own)], axis=1
        )

    own_terms, other_terms, w_gate_up = lax.optimization_barrier(
        (own_terms, other_terms, w_gate_up)
    )
    gate_up_weight = w_gate_up[0].reshape(model_width, 2 * ff_local)
    gots = [
        lax.ppermute(term(step).astype(bf16), "donor", rotation(n_donor, step)) for step in steps
    ]
    gots, gate_up_weight = lax.optimization_barrier((gots, gate_up_weight))
    total = term(0) + hidden_part.astype(f32)
    for got in gots:
        total = total + got.astype(f32)
    chunk = total.astype(bf16)

    all_gates = jnp.stack([pick(table, my_expert) for table in tables], axis=0)

    def core_gates(which):
        rows = [pick(all_gates, (expert_index - 2 * r - which) % n_expert) for r in range(n_rows)]
        return jnp.concatenate(rows).reshape(n_donor, part_rows)

    own_gates, other_gates = core_gates(core), core_gates(1 - core)

    gain_f = norm_gain.astype(f32)
    resid_parts = [None] * n_donor
    own_act, other_act = [None] * n_donor, [None] * n_donor
    batches = [max(1, n_donor - 1), 1]
    own_rows, other_rows, row_gates = [], [], []
    for slot in range(n_donor):
        part = (z - slot) % n_donor
        gots = [lax.ppermute(chunk, "expert", turn(hop)) for hop in range(1, n_rows)]
        here = chunk
        if slot < n_donor - 1:
            chunk = lax.ppermute(chunk, "donor", rotation(n_donor, 1))
            chunk, gots, other_rows[:-1] = lax.optimization_barrier((chunk, gots, other_rows[:-1]))
        if slot == n_donor - 1 and slot > 0:
            gots, own_act[:slot], other_act[:slot] = lax.optimization_barrier(
                (gots, own_act[:slot], other_act[:slot])
            )
        if n_rows == 2:
            block = jnp.concatenate(
                [jnp.where(y == 0, here, gots[0]), jnp.where(y == 0, gots[0], here)], axis=1
            )
        else:
            block = jnp.zeros((part_rows, n_rows, pair_cols), bf16)
            block = lax.dynamic_update_index_in_dim(block, here, y, 1)
            for hop, got in enumerate(gots, 1):
                block = lax.dynamic_update_index_in_dim(block, got, (y - hop) % n_rows, 1)
            block = block.reshape(part_rows, model_width)
        resid_parts[slot] = lax.dynamic_slice_in_dim(block, z * columns, columns, 1)
        block_f = block.astype(f32)
        inverse = lax.rsqrt(jnp.mean(block_f * block_f, axis=1, keepdims=True) + 1e-06)
        normed = (block_f * inverse * gain_f[None, :]).astype(bf16)
        own_rows.append(normed)
        other_rows.append(lax.ppermute(normed, "expert", swap))
        row_gates.append((pick(own_gates, part), pick(other_gates, part)))
        if len(row_gates) == batches[0]:
            batch = batches.pop(0)
            rows_in = jnp.concatenate(own_rows + other_rows, axis=0)
            scale = jnp.concatenate([g[0] for g in row_gates] + [g[1] for g in row_gates])
            gate_up = jnp.dot(rows_in, gate_up_weight, preferred_element_type=f32)
            act = jax.nn.silu(gate_up[:, :ff_local]) * gate_up[:, ff_local:]
            act = (act * scale[:, None]).astype(bf16).reshape(2, batch, part_rows, ff_local)
            for i in range(batch):
                own_act[slot - batch + 1 + i] = act[0, i]
                other_act[slot - batch + 1 + i] = act[1, i]
            own_rows, other_rows, row_gates = [], [], []

    def by_sequence(parts, rows):
        stacked = jnp.stack(parts, axis=0)
        return jnp.concatenate(
            [
                pick(stacked, (z - (y + r) % n_rows * parts_per_seq - i) % n_donor)
                for r in range(rows)
                for i in range(parts_per_seq)
            ],
            axis=0,
        )

    act_rows = jnp.concatenate(
        [by_sequence(other_act, n_rows), by_sequence(own_act, n_rows)], axis=0
    )
    half_rows = n_rows * suffix_len
    resid = by_sequence(resid_parts, 1).astype(f32)

    order = steps[::-1] + [0]
    pending, before = [], []
    for place, step in enumerate(order):
        if place == 2:
            act_rows = after(act_rows, *pending[0][1])
        down = lax.dynamic_slice_in_dim(w_down[0], (z + step) % n_donor * columns, columns, 1)
        mixed = jnp.dot(act_rows, down, preferred_element_type=f32)
        got = lax.ppermute(mixed[:half_rows].astype(bf16), "expert", swap)
        block = mixed[half_rows:] + after(got, *before).astype(f32)
        before = [block]
        block = block.reshape(n_rows, suffix_len, columns)
        arriving = [
            lax.ppermute(block[hop].astype(bf16), "expert", turn(hop)) for hop in range(1, n_rows)
        ]
        pending.append((block[0], arriving))
    total = resid
    carry = {1: [], -1: []}
    before = []
    for place, step in enumerate(order):
        part_sum, arriving = pending[place]
        part_sum = after(part_sum, *before)
        for got in arriving:
            part_sum = part_sum + got.astype(f32)
        before = [part_sum]
        if step:
            way = 1 if step <= n_donor // 2 else -1
            for got in carry[way]:
                part_sum = part_sum + got.astype(f32)
            carry[way] = [lax.ppermute(part_sum.astype(bf16), "donor", rotation(n_donor, way))]
        else:
            total = total + part_sum
    for got in carry[1] + carry[-1]:
        total = total + got.astype(f32)
    return (total.astype(bf16), head_out)


def solution(mesh):
    in_specs = (
        P(("groups", "expert"), None),
        P(("groups", "expert"), "donor"),
        P(("groups", "expert"), None, None),
        P(("groups", "expert", "donor"), None, None, None),
        P("groups", None),
        P("groups"),
        P("donor", "expert"),
        P(),
        P(("groups", "expert"), None),
        P(("groups", "expert"), None),
        P(("expert", "donor"), None, None, None),
        P(("expert", "donor"), None, None),
    )
    out_specs = (P(("groups", "expert"), "donor"), P(("groups", "expert"), "donor"))
    return jax.shard_map(shards, mesh=mesh, in_specs=in_specs, out_specs=out_specs, check_vma=False)
```

```python
import jax
import jax.numpy as jnp
from jax import lax
from jax.sharding import PartitionSpec as P


def rotation(count, step):
    return [(i, (i + step) % count) for i in range(count)]


def pick(array, index, axis=0):
    return lax.dynamic_index_in_dim(array, index, axis, keepdims=False)


def after(array, *others):
    return lax.optimization_barrier((array, *others))[0]


def attention(queries, suffix_kv, kv_pool, page_table, prefix_len):
    n_expert = lax.axis_size("expert")
    n_donor = lax.axis_size("donor")
    expert_index = lax.axis_index("expert")
    donor_index = lax.axis_index("donor")
    seq_count, page_count = page_table.shape
    suffix_len = queries.shape[0]
    kv_heads = suffix_kv.shape[1]
    head_dim = suffix_kv.shape[2] // 2
    page_len = kv_pool.shape[2]
    my_group = donor_index * kv_heads // n_donor
    owner_index = expert_index * n_donor + donor_index
    owner_of = page_table // seq_count
    held_slot = jnp.sum(jnp.where(owner_of == owner_index, page_table % seq_count, 0), axis=1)
    dest_group = jnp.arange(n_donor, dtype=jnp.int32) * kv_heads // n_donor
    wanted = (held_slot[:, None] * kv_heads + dest_group[None, :]).reshape(-1)
    outgoing = jnp.take(
        kv_pool.reshape(seq_count * kv_heads, page_len, 2 * head_dim), wanted, axis=0
    )
    arrived = lax.all_to_all(outgoing, ("expert", "donor"), split_axis=0, concat_axis=0, tiled=True)
    my_owners = lax.dynamic_index_in_dim(owner_of, expert_index, 0, keepdims=False)
    ordered = jnp.take(arrived, my_owners, axis=0).reshape(page_count * page_len, 2 * head_dim)
    prefix_keys = ordered[:, :head_dim]
    prefix_vals = ordered[:, head_dim:]
    score_scale = head_dim ** (-0.5)
    query_heads = queries.reshape(suffix_len, -1, head_dim)
    fresh_pair = lax.dynamic_index_in_dim(suffix_kv, my_group, 1, keepdims=False)
    causal = jnp.arange(suffix_len)[:, None] >= jnp.arange(suffix_len)[None, :]
    fresh_scores = (
        jnp.einsum(
            "thc,uc->thu", query_heads, fresh_pair[:, :head_dim], preferred_element_type=jnp.float32
        )
        * score_scale
    )
    fresh_scores = jnp.where(causal[:, None, :], fresh_scores, -jnp.inf)
    prefix_tokens = lax.dynamic_index_in_dim(prefix_len, expert_index, 0, keepdims=False)
    block_keys = min(1024, page_count * page_len)
    live_blocks = (prefix_tokens + block_keys - 1) // block_keys

    def block_scores(block_index):
        keys_block = lax.dynamic_slice_in_dim(prefix_keys, block_index * block_keys, block_keys, 0)
        raw_scores = (
            jnp.einsum("thc,kc->thk", query_heads, keys_block, preferred_element_type=jnp.float32)
            * score_scale
        )
        visible = block_index * block_keys + jnp.arange(block_keys) < prefix_tokens
        return jnp.where(visible[None, None, :], raw_scores, -jnp.inf)

    def raise_max(block_index, running):
        return jnp.maximum(running, jnp.max(block_scores(block_index), axis=2))

    row_max = lax.fori_loop(0, live_blocks, raise_max, jnp.max(fresh_scores, axis=2))

    def add_block(block_index, loop_state):
        row_total, weighted = loop_state
        exp_scores = jnp.exp(block_scores(block_index) - row_max[:, :, None])
        vals_block = lax.dynamic_slice_in_dim(prefix_vals, block_index * block_keys, block_keys, 0)
        weighted = weighted + jnp.einsum(
            "thk,kc->thc",
            exp_scores.astype(jnp.bfloat16),
            vals_block,
            preferred_element_type=jnp.float32,
        )
        return (row_total + jnp.sum(exp_scores, axis=2), weighted)

    fresh_exp = jnp.exp(fresh_scores - row_max[:, :, None])
    start_state = (
        jnp.sum(fresh_exp, axis=2),
        jnp.einsum(
            "thu,uc->thc",
            fresh_exp.astype(jnp.bfloat16),
            fresh_pair[:, head_dim:],
            preferred_element_type=jnp.float32,
        ),
    )
    row_total, weighted = lax.fori_loop(0, live_blocks, add_block, start_state)
    return (weighted / row_total[:, :, None]).astype(jnp.bfloat16).reshape(suffix_len, -1)


def shards(
    hidden_in,
    queries,
    suffix_kv,
    kv_pool,
    page_table,
    prefix_len,
    out_weight,
    norm_gain,
    expert_ids,
    route_probs,
    w_gate_up,
    w_down,
):
    f32, bf16 = jnp.float32, jnp.bfloat16
    n_expert = lax.axis_size("expert")
    n_donor = lax.axis_size("donor")
    expert_index = lax.axis_index("expert")
    z = lax.axis_index("donor")
    n_rows = n_expert // 2
    y = expert_index // 2
    core = expert_index % 2
    swap = [(i, i ^ 1) for i in range(n_expert)]

    def turn(step):
        return rotation(n_expert, 2 * step)

    suffix_len, model_width = hidden_in.shape
    experts_all = 2 * n_expert
    ff_local = w_gate_up.shape[3]
    share_count = n_donor // 2
    my_expert = 2 * expert_index + z // share_count
    pair_cols = model_width // n_rows
    part_rows = n_rows * suffix_len // n_donor
    parts_per_seq = suffix_len // part_rows
    columns = model_width // n_donor
    steps = sorted(range(1, n_donor), key=lambda step: min(step, n_donor - step))

    gates = route_probs / jnp.sum(route_probs, axis=1, keepdims=True)
    hits = expert_ids[:, :, None] == jnp.arange(experts_all, dtype=jnp.int32)
    gate_table = jnp.sum(jnp.where(hits, gates[:, :, None], 0.0), axis=1).T
    tables = [gate_table] + [
        lax.ppermute(gate_table, "expert", rotation(n_expert, step)) for step in range(1, n_expert)
    ]

    other_weight = lax.ppermute(out_weight, "expert", swap)

    part_owner = z * part_rows // suffix_len
    hidden_rows = lax.dynamic_slice_in_dim(hidden_in, z * part_rows % suffix_len, part_rows, 0)

    def hidden_block(row):
        return lax.dynamic_slice_in_dim(hidden_rows, row * pair_cols, pair_cols, 1)

    hidden_part = hidden_block(y)
    for step in range(1, n_rows):
        got = lax.ppermute(hidden_block((y + step) % n_rows), "expert", turn(step))
        hidden_part = jnp.where((y - step) % n_rows == part_owner, got, hidden_part)

    head_out = attention(queries, suffix_kv, kv_pool, page_table, prefix_len)

    heads = jnp.zeros((n_rows, suffix_len, head_out.shape[1]), bf16)
    heads = lax.dynamic_update_index_in_dim(heads, head_out, y, 0)
    for step in range(1, n_rows):
        got = lax.ppermute(head_out, "expert", turn(step))
        got, tables = lax.optimization_barrier((got, tables))
        heads = lax.dynamic_update_index_in_dim(heads, got, (y - step) % n_rows, 0)
    heads = heads.reshape(n_donor, part_rows, -1)
    heads = jnp.concatenate([pick(heads, (z + step) % n_donor) for step in range(n_donor)])
    own_terms = jnp.dot(heads, out_weight, preferred_element_type=f32)
    other_terms = jnp.dot(heads, other_weight, preferred_element_type=f32)

    def term(step):
        rows = slice(step * part_rows, (step + 1) * part_rows)
        own, other = own_terms[rows], other_terms[rows]
        return jnp.concatenate(
            [jnp.where(core == 0, own, other), jnp.where(core == 0, other, own)], axis=1
        )

    own_terms, other_terms, w_gate_up = lax.optimization_barrier(
        (own_terms, other_terms, w_gate_up)
    )
    gate_up_weight = w_gate_up[0].reshape(model_width, 2 * ff_local)
    gots = [
        lax.ppermute(term(step).astype(bf16), "donor", rotation(n_donor, step)) for step in steps
    ]
    gots, gate_up_weight = lax.optimization_barrier((gots, gate_up_weight))
    total = term(0) + hidden_part.astype(f32)
    for got in gots:
        total = total + got.astype(f32)
    chunk = total.astype(bf16)

    all_gates = jnp.stack([pick(table, my_expert) for table in tables], axis=0)

    def core_gates(which):
        rows = [pick(all_gates, (expert_index - 2 * r - which) % n_expert) for r in range(n_rows)]
        return jnp.concatenate(rows).reshape(n_donor, part_rows)

    own_gates, other_gates = core_gates(core), core_gates(1 - core)

    gain_f = norm_gain.astype(f32)
    resid_parts = [None] * n_donor
    own_act, other_act = [None] * n_donor, [None] * n_donor
    batches = [n_donor // 2, n_donor - n_donor // 2]
    own_rows, other_rows, row_gates = [], [], []
    for slot in range(n_donor):
        part = (z - slot) % n_donor
        gots = [lax.ppermute(chunk, "expert", turn(hop)) for hop in range(1, n_rows)]
        here = chunk
        if slot < n_donor - 1:
            chunk = lax.ppermute(chunk, "donor", rotation(n_donor, 1))
            chunk, gots, other_rows[:-1] = lax.optimization_barrier((chunk, gots, other_rows[:-1]))
        if slot == n_donor - 1 and slot > 0:
            gots, own_act[:slot], other_act[:slot] = lax.optimization_barrier(
                (gots, own_act[:slot], other_act[:slot])
            )
        if n_rows == 2:
            block = jnp.concatenate(
                [jnp.where(y == 0, here, gots[0]), jnp.where(y == 0, gots[0], here)], axis=1
            )
        else:
            block = jnp.zeros((part_rows, n_rows, pair_cols), bf16)
            block = lax.dynamic_update_index_in_dim(block, here, y, 1)
            for hop, got in enumerate(gots, 1):
                block = lax.dynamic_update_index_in_dim(block, got, (y - hop) % n_rows, 1)
            block = block.reshape(part_rows, model_width)
        resid_parts[slot] = lax.dynamic_slice_in_dim(block, z * columns, columns, 1)
        block_f = block.astype(f32)
        inverse = lax.rsqrt(jnp.mean(block_f * block_f, axis=1, keepdims=True) + 1e-06)
        normed = (block_f * inverse * gain_f[None, :]).astype(bf16)
        own_rows.append(normed)
        other_rows.append(lax.ppermute(normed, "expert", swap))
        row_gates.append((pick(own_gates, part), pick(other_gates, part)))
        if len(row_gates) == batches[0]:
            batch = batches.pop(0)
            rows_in = jnp.concatenate(own_rows + other_rows, axis=0)
            scale = jnp.concatenate([g[0] for g in row_gates] + [g[1] for g in row_gates])
            gate_up = jnp.dot(rows_in, gate_up_weight, preferred_element_type=f32)
            act = jax.nn.silu(gate_up[:, :ff_local]) * gate_up[:, ff_local:]
            act = (act * scale[:, None]).astype(bf16).reshape(2, batch, part_rows, ff_local)
            for i in range(batch):
                own_act[slot - batch + 1 + i] = act[0, i]
                other_act[slot - batch + 1 + i] = act[1, i]
            own_rows, other_rows, row_gates = [], [], []

    def by_sequence(parts, rows):
        stacked = jnp.stack(parts, axis=0)
        return jnp.concatenate(
            [
                pick(stacked, (z - (y + r) % n_rows * parts_per_seq - i) % n_donor)
                for r in range(rows)
                for i in range(parts_per_seq)
            ],
            axis=0,
        )

    act_rows = jnp.concatenate(
        [by_sequence(other_act, n_rows), by_sequence(own_act, n_rows)], axis=0
    )
    half_rows = n_rows * suffix_len
    resid = by_sequence(resid_parts, 1).astype(f32)

    order = steps[::-1] + [0]
    pending, before = [], []
    for place, step in enumerate(order):
        if place == 2:
            act_rows = after(act_rows, *pending[0][1])
        down = lax.dynamic_slice_in_dim(w_down[0], (z + step) % n_donor * columns, columns, 1)
        mixed = jnp.dot(act_rows, down, preferred_element_type=f32)
        got = lax.ppermute(mixed[:half_rows].astype(bf16), "expert", swap)
        block = mixed[half_rows:] + after(got, *before).astype(f32)
        before = [block]
        block = block.reshape(n_rows, suffix_len, columns)
        arriving = [
            lax.ppermute(block[hop].astype(bf16), "expert", turn(hop)) for hop in range(1, n_rows)
        ]
        pending.append((block[0], arriving))
    total = resid
    carry = {1: [], -1: []}
    all_blocks, before = before, []
    for place, step in enumerate(order):
        part_sum, arriving = pending[place]
        part_sum = after(part_sum, *before)
        for got in arriving:
            part_sum = part_sum + got.astype(f32)
        before = [part_sum] + all_blocks
        if step:
            way = 1 if step <= n_donor // 2 else -1
            for got in carry[way]:
                part_sum = part_sum + got.astype(f32)
            carry[way] = [lax.ppermute(part_sum.astype(bf16), "donor", rotation(n_donor, way))]
        else:
            total = total + part_sum
    for got in carry[1] + carry[-1]:
        total = total + got.astype(f32)
    return (total.astype(bf16), head_out)


def solution(mesh):
    in_specs = (
        P(("groups", "expert"), None),
        P(("groups", "expert"), "donor"),
        P(("groups", "expert"), None, None),
        P(("groups", "expert", "donor"), None, None, None),
        P("groups", None),
        P("groups"),
        P("donor", "expert"),
        P(),
        P(("groups", "expert"), None),
        P(("groups", "expert"), None),
        P(("expert", "donor"), None, None, None),
        P(("expert", "donor"), None, None),
    )
    out_specs = (P(("groups", "expert"), "donor"), P(("groups", "expert"), "donor"))
    return jax.shard_map(shards, mesh=mesh, in_specs=in_specs, out_specs=out_specs, check_vma=False)
```

```python
import jax
import jax.numpy as jnp
from jax import lax
from jax.sharding import PartitionSpec as P


def rotation(count, step):
    return [(i, (i + step) % count) for i in range(count)]


def pick(array, index, axis=0):
    return lax.dynamic_index_in_dim(array, index, axis, keepdims=False)


def after(array, *others):
    return lax.optimization_barrier((array, *others))[0]


def attention(queries, suffix_kv, kv_pool, page_table, prefix_len):
    n_expert = lax.axis_size("expert")
    n_donor = lax.axis_size("donor")
    expert_index = lax.axis_index("expert")
    donor_index = lax.axis_index("donor")
    seq_count, page_count = page_table.shape
    suffix_len = queries.shape[0]
    kv_heads = suffix_kv.shape[1]
    head_dim = suffix_kv.shape[2] // 2
    page_len = kv_pool.shape[2]
    my_group = donor_index * kv_heads // n_donor
    owner_index = expert_index * n_donor + donor_index
    owner_of = page_table // seq_count
    held_slot = jnp.sum(jnp.where(owner_of == owner_index, page_table % seq_count, 0), axis=1)
    dest_group = jnp.arange(n_donor, dtype=jnp.int32) * kv_heads // n_donor
    wanted = (held_slot[:, None] * kv_heads + dest_group[None, :]).reshape(-1)
    outgoing = jnp.take(
        kv_pool.reshape(seq_count * kv_heads, page_len, 2 * head_dim), wanted, axis=0
    )
    arrived = lax.all_to_all(outgoing, ("expert", "donor"), split_axis=0, concat_axis=0, tiled=True)
    my_owners = lax.dynamic_index_in_dim(owner_of, expert_index, 0, keepdims=False)
    ordered = jnp.take(arrived, my_owners, axis=0).reshape(page_count * page_len, 2 * head_dim)
    prefix_keys = ordered[:, :head_dim]
    prefix_vals = ordered[:, head_dim:]
    score_scale = head_dim ** (-0.5)
    query_heads = queries.reshape(suffix_len, -1, head_dim)
    fresh_pair = lax.dynamic_index_in_dim(suffix_kv, my_group, 1, keepdims=False)
    causal = jnp.arange(suffix_len)[:, None] >= jnp.arange(suffix_len)[None, :]
    fresh_scores = (
        jnp.einsum(
            "thc,uc->thu", query_heads, fresh_pair[:, :head_dim], preferred_element_type=jnp.float32
        )
        * score_scale
    )
    fresh_scores = jnp.where(causal[:, None, :], fresh_scores, -jnp.inf)
    prefix_tokens = lax.dynamic_index_in_dim(prefix_len, expert_index, 0, keepdims=False)
    block_keys = min(1024, page_count * page_len)
    live_blocks = (prefix_tokens + block_keys - 1) // block_keys

    def block_scores(block_index):
        keys_block = lax.dynamic_slice_in_dim(prefix_keys, block_index * block_keys, block_keys, 0)
        raw_scores = (
            jnp.einsum("thc,kc->thk", query_heads, keys_block, preferred_element_type=jnp.float32)
            * score_scale
        )
        visible = block_index * block_keys + jnp.arange(block_keys) < prefix_tokens
        return jnp.where(visible[None, None, :], raw_scores, -jnp.inf)

    def raise_max(block_index, running):
        return jnp.maximum(running, jnp.max(block_scores(block_index), axis=2))

    row_max = lax.fori_loop(0, live_blocks, raise_max, jnp.max(fresh_scores, axis=2))

    def add_block(block_index, loop_state):
        row_total, weighted = loop_state
        exp_scores = jnp.exp(block_scores(block_index) - row_max[:, :, None])
        vals_block = lax.dynamic_slice_in_dim(prefix_vals, block_index * block_keys, block_keys, 0)
        weighted = weighted + jnp.einsum(
            "thk,kc->thc",
            exp_scores.astype(jnp.bfloat16),
            vals_block,
            preferred_element_type=jnp.float32,
        )
        return (row_total + jnp.sum(exp_scores, axis=2), weighted)

    fresh_exp = jnp.exp(fresh_scores - row_max[:, :, None])
    start_state = (
        jnp.sum(fresh_exp, axis=2),
        jnp.einsum(
            "thu,uc->thc",
            fresh_exp.astype(jnp.bfloat16),
            fresh_pair[:, head_dim:],
            preferred_element_type=jnp.float32,
        ),
    )
    row_total, weighted = lax.fori_loop(0, live_blocks, add_block, start_state)
    return (weighted / row_total[:, :, None]).astype(jnp.bfloat16).reshape(suffix_len, -1)


def shards(
    hidden_in,
    queries,
    suffix_kv,
    kv_pool,
    page_table,
    prefix_len,
    out_weight,
    norm_gain,
    expert_ids,
    route_probs,
    w_gate_up,
    w_down,
):
    f32, bf16 = jnp.float32, jnp.bfloat16
    n_expert = lax.axis_size("expert")
    n_donor = lax.axis_size("donor")
    expert_index = lax.axis_index("expert")
    z = lax.axis_index("donor")
    n_rows = n_expert // 2
    y = expert_index // 2
    core = expert_index % 2
    swap = [(i, i ^ 1) for i in range(n_expert)]

    def turn(step):
        return rotation(n_expert, 2 * step)

    suffix_len, model_width = hidden_in.shape
    experts_all = 2 * n_expert
    ff_local = w_gate_up.shape[3]
    share_count = n_donor // 2
    my_expert = 2 * expert_index + z // share_count
    pair_cols = model_width // n_rows
    part_rows = n_rows * suffix_len // n_donor
    parts_per_seq = suffix_len // part_rows
    columns = model_width // n_donor
    steps = sorted(range(1, n_donor), key=lambda step: min(step, n_donor - step))

    gates = route_probs / jnp.sum(route_probs, axis=1, keepdims=True)
    hits = expert_ids[:, :, None] == jnp.arange(experts_all, dtype=jnp.int32)
    gate_table = jnp.sum(jnp.where(hits, gates[:, :, None], 0.0), axis=1).T
    tables = [gate_table] + [
        lax.ppermute(gate_table, "expert", rotation(n_expert, step)) for step in range(1, n_expert)
    ]

    other_weight = lax.ppermute(out_weight, "expert", swap)

    part_owner = z * part_rows // suffix_len
    hidden_rows = lax.dynamic_slice_in_dim(hidden_in, z * part_rows % suffix_len, part_rows, 0)

    def hidden_block(row):
        return lax.dynamic_slice_in_dim(hidden_rows, row * pair_cols, pair_cols, 1)

    hidden_part = hidden_block(y)
    for step in range(1, n_rows):
        got = lax.ppermute(hidden_block((y + step) % n_rows), "expert", turn(step))
        hidden_part = jnp.where((y - step) % n_rows == part_owner, got, hidden_part)

    head_out = attention(queries, suffix_kv, kv_pool, page_table, prefix_len)

    heads = jnp.zeros((n_rows, suffix_len, head_out.shape[1]), bf16)
    heads = lax.dynamic_update_index_in_dim(heads, head_out, y, 0)
    for step in range(1, n_rows):
        got = lax.ppermute(head_out, "expert", turn(step))
        got, tables = lax.optimization_barrier((got, tables))
        heads = lax.dynamic_update_index_in_dim(heads, got, (y - step) % n_rows, 0)
    heads = heads.reshape(n_donor, part_rows, -1)
    heads = jnp.concatenate([pick(heads, (z + step) % n_donor) for step in range(n_donor)])
    own_terms = jnp.dot(heads, out_weight, preferred_element_type=f32)
    other_terms = jnp.dot(heads, other_weight, preferred_element_type=f32)

    def term(step):
        rows = slice(step * part_rows, (step + 1) * part_rows)
        own, other = own_terms[rows], other_terms[rows]
        return jnp.concatenate(
            [jnp.where(core == 0, own, other), jnp.where(core == 0, other, own)], axis=1
        )

    own_terms, other_terms, w_gate_up = lax.optimization_barrier(
        (own_terms, other_terms, w_gate_up)
    )
    weights = [
        w_gate_up[0, row * pair_cols : (row + 1) * pair_cols].reshape(pair_cols, 2 * ff_local)
        for row in range(n_rows)
    ]
    early = n_rows // 2
    carry = {1: [], -1: []}
    for place, step in enumerate(steps[::-1]):
        way = 1 if step <= n_donor // 2 else -1
        part = term(step)
        for got in carry[way]:
            part = part + got.astype(f32)
        got = lax.ppermute(part.astype(bf16), "donor", rotation(n_donor, way))
        if place == 0:
            got, weights[:early] = lax.optimization_barrier((got, weights[:early]))
        if place == n_donor - 2:
            got, weights[early:] = lax.optimization_barrier((got, weights[early:]))
        carry[way] = [got]
    total = term(0) + hidden_part.astype(f32)
    for got in carry[1] + carry[-1]:
        total = total + got.astype(f32)
    chunk = total.astype(bf16)

    all_gates = jnp.stack([pick(table, my_expert) for table in tables], axis=0)

    def core_gates(which):
        rows = [pick(all_gates, (expert_index - 2 * r - which) % n_expert) for r in range(n_rows)]
        return jnp.concatenate(rows).reshape(n_donor, part_rows)

    own_gates, other_gates = core_gates(core), core_gates(1 - core)

    gain_f = norm_gain.astype(f32)
    resid_parts = [None] * n_donor
    own_act, other_act = [None] * n_donor, [None] * n_donor
    batches = [n_donor // 2, n_donor - n_donor // 2]
    own_rows, other_rows, row_gates = [], [], []
    for slot in range(n_donor):
        part = (z - slot) % n_donor
        gots = [lax.ppermute(chunk, "expert", turn(hop)) for hop in range(1, n_rows)]
        here = chunk
        if slot < n_donor - 1:
            chunk = lax.ppermute(chunk, "donor", rotation(n_donor, 1))
            chunk, gots, other_rows[:-1] = lax.optimization_barrier((chunk, gots, other_rows[:-1]))
        if slot == n_donor - 1 and slot > 0:
            gots, own_act[:slot], other_act[:slot] = lax.optimization_barrier(
                (gots, own_act[:slot], other_act[:slot])
            )
        if n_rows == 2:
            pieces = [jnp.where(y == 0, here, gots[0]), jnp.where(y == 0, gots[0], here)]
        else:
            stacked = jnp.stack([here] + gots, axis=0)
            pieces = [pick(stacked, (y - row) % n_rows) for row in range(n_rows)]
        block = jnp.concatenate(pieces, axis=1)
        resid_parts[slot] = lax.dynamic_slice_in_dim(block, z * columns, columns, 1)
        pieces = [piece.astype(f32) for piece in pieces]
        squares = sum(jnp.sum(piece * piece, axis=1, keepdims=True) for piece in pieces)
        inverse = lax.rsqrt(squares / model_width + 1e-06)
        normed = jnp.stack(
            [
                (piece * inverse * gain_f[None, row * pair_cols : (row + 1) * pair_cols]).astype(bf16)
                for row, piece in enumerate(pieces)
            ],
            axis=0,
        )
        own_rows.append(normed)
        other_rows.append(lax.ppermute(normed, "expert", swap))
        row_gates.append((pick(own_gates, part), pick(other_gates, part)))
        if len(row_gates) == batches[0]:
            batch = batches.pop(0)
            scale = jnp.concatenate([g[0] for g in row_gates] + [g[1] for g in row_gates])
            gate_up = sum(
                jnp.dot(
                    jnp.concatenate([rows[row] for rows in own_rows + other_rows], axis=0),
                    weights[row],
                    preferred_element_type=f32,
                )
                for row in range(n_rows)
            )
            act = jax.nn.silu(gate_up[:, :ff_local]) * gate_up[:, ff_local:]
            act = (act * scale[:, None]).astype(bf16).reshape(2, batch, part_rows, ff_local)
            for i in range(batch):
                own_act[slot - batch + 1 + i] = act[0, i]
                other_act[slot - batch + 1 + i] = act[1, i]
            own_rows, other_rows, row_gates = [], [], []

    def by_sequence(parts, rows):
        stacked = jnp.stack(parts, axis=0)
        return jnp.concatenate(
            [
                pick(stacked, (z - (y + r) % n_rows * parts_per_seq - i) % n_donor)
                for r in range(rows)
                for i in range(parts_per_seq)
            ],
            axis=0,
        )

    act_rows = jnp.concatenate(
        [by_sequence(other_act, n_rows), by_sequence(own_act, n_rows)], axis=0
    )
    half_rows = n_rows * suffix_len
    resid = by_sequence(resid_parts, 1).astype(f32)

    order = steps[::-1] + [0]
    pending, before = [], []
    for place, step in enumerate(order):
        if place == 2:
            act_rows = after(act_rows, *pending[0][1])
        down = lax.dynamic_slice_in_dim(w_down[0], (z + step) % n_donor * columns, columns, 1)
        mixed = jnp.dot(act_rows, down, preferred_element_type=f32)
        got = lax.ppermute(mixed[:half_rows].astype(bf16), "expert", swap)
        block = mixed[half_rows:] + after(got, *before).astype(f32)
        before = [block]
        block = block.reshape(n_rows, suffix_len, columns)
        arriving = [
            lax.ppermute(block[hop].astype(bf16), "expert", turn(hop)) for hop in range(1, n_rows)
        ]
        pending.append((block[0], arriving))
    total = resid
    carry = {1: [], -1: []}
    all_blocks, before = before, []
    for place, step in enumerate(order):
        part_sum, arriving = pending[place]
        part_sum = after(part_sum, *before)
        for got in arriving:
            part_sum = part_sum + got.astype(f32)
        before = [part_sum] + all_blocks
        if step:
            way = 1 if step <= n_donor // 2 else -1
            for got in carry[way]:
                part_sum = part_sum + got.astype(f32)
            carry[way] = [lax.ppermute(part_sum.astype(bf16), "donor", rotation(n_donor, way))]
        else:
            total = total + part_sum
    for got in carry[1] + carry[-1]:
        total = total + got.astype(f32)
    return (total.astype(bf16), head_out)


def solution(mesh):
    in_specs = (
        P(("groups", "expert"), None),
        P(("groups", "expert"), "donor"),
        P(("groups", "expert"), None, None),
        P(("groups", "expert", "donor"), None, None, None),
        P("groups", None),
        P("groups"),
        P("donor", "expert"),
        P(),
        P(("groups", "expert"), None),
        P(("groups", "expert"), None),
        P(("expert", "donor"), None, None, None),
        P(("expert", "donor"), None, None),
    )
    out_specs = (P(("groups", "expert"), "donor"), P(("groups", "expert"), "donor"))
    return jax.shard_map(shards, mesh=mesh, in_specs=in_specs, out_specs=out_specs, check_vma=False)
```

```python
import jax
import jax.numpy as jnp
from jax import lax
from jax.sharding import PartitionSpec as P


def rotation(count, step):
    return [(i, (i + step) % count) for i in range(count)]


def pick(array, index, axis=0):
    return lax.dynamic_index_in_dim(array, index, axis, keepdims=False)


def after(array, *others):
    return lax.optimization_barrier((array, *others))[0]


def attention(queries, suffix_kv, kv_pool, page_table, prefix_len):
    n_expert = lax.axis_size("expert")
    n_donor = lax.axis_size("donor")
    expert_index = lax.axis_index("expert")
    donor_index = lax.axis_index("donor")
    seq_count, page_count = page_table.shape
    suffix_len = queries.shape[0]
    kv_heads = suffix_kv.shape[1]
    head_dim = suffix_kv.shape[2] // 2
    page_len = kv_pool.shape[2]
    my_group = donor_index * kv_heads // n_donor
    owner_index = expert_index * n_donor + donor_index
    owner_of = page_table // seq_count
    held_slot = jnp.sum(jnp.where(owner_of == owner_index, page_table % seq_count, 0), axis=1)
    dest_group = jnp.arange(n_donor, dtype=jnp.int32) * kv_heads // n_donor
    wanted = (held_slot[:, None] * kv_heads + dest_group[None, :]).reshape(-1)
    outgoing = jnp.take(
        kv_pool.reshape(seq_count * kv_heads, page_len, 2 * head_dim), wanted, axis=0
    )
    arrived = lax.all_to_all(outgoing, ("expert", "donor"), split_axis=0, concat_axis=0, tiled=True)
    my_owners = lax.dynamic_index_in_dim(owner_of, expert_index, 0, keepdims=False)
    ordered = jnp.take(arrived, my_owners, axis=0).reshape(page_count * page_len, 2 * head_dim)
    prefix_keys = ordered[:, :head_dim]
    prefix_vals = ordered[:, head_dim:]
    score_scale = head_dim ** (-0.5)
    query_heads = queries.reshape(suffix_len, -1, head_dim)
    fresh_pair = lax.dynamic_index_in_dim(suffix_kv, my_group, 1, keepdims=False)
    causal = jnp.arange(suffix_len)[:, None] >= jnp.arange(suffix_len)[None, :]
    fresh_scores = (
        jnp.einsum(
            "thc,uc->thu", query_heads, fresh_pair[:, :head_dim], preferred_element_type=jnp.float32
        )
        * score_scale
    )
    fresh_scores = jnp.where(causal[:, None, :], fresh_scores, -jnp.inf)
    prefix_tokens = lax.dynamic_index_in_dim(prefix_len, expert_index, 0, keepdims=False)
    block_keys = min(1024, page_count * page_len)
    live_blocks = (prefix_tokens + block_keys - 1) // block_keys

    def block_scores(block_index):
        keys_block = lax.dynamic_slice_in_dim(prefix_keys, block_index * block_keys, block_keys, 0)
        raw_scores = (
            jnp.einsum("thc,kc->thk", query_heads, keys_block, preferred_element_type=jnp.float32)
            * score_scale
        )
        visible = block_index * block_keys + jnp.arange(block_keys) < prefix_tokens
        return jnp.where(visible[None, None, :], raw_scores, -jnp.inf)

    def raise_max(block_index, running):
        return jnp.maximum(running, jnp.max(block_scores(block_index), axis=2))

    row_max = lax.fori_loop(0, live_blocks, raise_max, jnp.max(fresh_scores, axis=2))

    def add_block(block_index, loop_state):
        row_total, weighted = loop_state
        exp_scores = jnp.exp(block_scores(block_index) - row_max[:, :, None])
        vals_block = lax.dynamic_slice_in_dim(prefix_vals, block_index * block_keys, block_keys, 0)
        weighted = weighted + jnp.einsum(
            "thk,kc->thc",
            exp_scores.astype(jnp.bfloat16),
            vals_block,
            preferred_element_type=jnp.float32,
        )
        return (row_total + jnp.sum(exp_scores, axis=2), weighted)

    fresh_exp = jnp.exp(fresh_scores - row_max[:, :, None])
    start_state = (
        jnp.sum(fresh_exp, axis=2),
        jnp.einsum(
            "thu,uc->thc",
            fresh_exp.astype(jnp.bfloat16),
            fresh_pair[:, head_dim:],
            preferred_element_type=jnp.float32,
        ),
    )
    row_total, weighted = lax.fori_loop(0, live_blocks, add_block, start_state)
    return (weighted / row_total[:, :, None]).astype(jnp.bfloat16).reshape(suffix_len, -1)


def shards(
    hidden_in,
    queries,
    suffix_kv,
    kv_pool,
    page_table,
    prefix_len,
    out_weight,
    norm_gain,
    expert_ids,
    route_probs,
    w_gate_up,
    w_down,
):
    f32, bf16 = jnp.float32, jnp.bfloat16
    n_expert = lax.axis_size("expert")
    n_donor = lax.axis_size("donor")
    expert_index = lax.axis_index("expert")
    z = lax.axis_index("donor")
    n_rows = n_expert // 2
    y = expert_index // 2
    core = expert_index % 2
    swap = [(i, i ^ 1) for i in range(n_expert)]

    def turn(step):
        return rotation(n_expert, 2 * step)

    suffix_len, model_width = hidden_in.shape
    experts_all = 2 * n_expert
    ff_local = w_gate_up.shape[3]
    share_count = n_donor // 2
    my_expert = 2 * expert_index + z // share_count
    pair_cols = model_width // n_rows
    part_rows = n_rows * suffix_len // n_donor
    parts_per_seq = suffix_len // part_rows
    columns = model_width // n_donor
    steps = sorted(range(1, n_donor), key=lambda step: min(step, n_donor - step))

    gates = route_probs / jnp.sum(route_probs, axis=1, keepdims=True)
    hits = expert_ids[:, :, None] == jnp.arange(experts_all, dtype=jnp.int32)
    gate_table = jnp.sum(jnp.where(hits, gates[:, :, None], 0.0), axis=1).T
    tables = [gate_table] + [
        lax.ppermute(gate_table, "expert", rotation(n_expert, step)) for step in range(1, n_expert)
    ]

    other_weight = lax.ppermute(out_weight, "expert", swap)

    part_owner = z * part_rows // suffix_len
    hidden_rows = lax.dynamic_slice_in_dim(hidden_in, z * part_rows % suffix_len, part_rows, 0)

    def hidden_block(row):
        return lax.dynamic_slice_in_dim(hidden_rows, row * pair_cols, pair_cols, 1)

    hidden_part = hidden_block(y)
    for step in range(1, n_rows):
        got = lax.ppermute(hidden_block((y + step) % n_rows), "expert", turn(step))
        hidden_part = jnp.where((y - step) % n_rows == part_owner, got, hidden_part)

    head_out = attention(queries, suffix_kv, kv_pool, page_table, prefix_len)

    heads = jnp.zeros((n_rows, suffix_len, head_out.shape[1]), bf16)
    heads = lax.dynamic_update_index_in_dim(heads, head_out, y, 0)
    for step in range(1, n_rows):
        got = lax.ppermute(head_out, "expert", turn(step))
        got, tables = lax.optimization_barrier((got, tables))
        heads = lax.dynamic_update_index_in_dim(heads, got, (y - step) % n_rows, 0)
    heads = heads.reshape(n_donor, part_rows, -1)
    heads = jnp.concatenate([pick(heads, (z + step) % n_donor) for step in range(n_donor)])
    own_terms = jnp.dot(heads, out_weight, preferred_element_type=f32)
    other_terms = jnp.dot(heads, other_weight, preferred_element_type=f32)

    def term(step):
        rows = slice(step * part_rows, (step + 1) * part_rows)
        own, other = own_terms[rows], other_terms[rows]
        return jnp.concatenate(
            [jnp.where(core == 0, own, other), jnp.where(core == 0, other, own)], axis=1
        )

    own_terms, other_terms, w_gate_up = lax.optimization_barrier(
        (own_terms, other_terms, w_gate_up)
    )
    gate_up_weight = w_gate_up[0].reshape(model_width, 2 * ff_local)
    gots = [
        lax.ppermute(term(step).astype(bf16), "donor", rotation(n_donor, step)) for step in steps
    ]
    gots, gate_up_weight = lax.optimization_barrier((gots, gate_up_weight))
    total = term(0) + hidden_part.astype(f32)
    for got in gots:
        total = total + got.astype(f32)
    chunk = total.astype(bf16)

    all_gates = jnp.stack([pick(table, my_expert) for table in tables], axis=0)

    def core_gates(which):
        rows = [pick(all_gates, (expert_index - 2 * r - which) % n_expert) for r in range(n_rows)]
        return jnp.concatenate(rows).reshape(n_donor, part_rows)

    own_gates, other_gates = core_gates(core), core_gates(1 - core)

    gain_f = norm_gain.astype(f32)
    resid_parts = [None] * n_donor
    own_act, other_act = [None] * n_donor, [None] * n_donor
    batches = [n_donor // 2, n_donor - n_donor // 2]
    own_rows, other_rows, row_gates = [], [], []
    for slot in range(n_donor):
        part = (z - slot) % n_donor
        gots = [lax.ppermute(chunk, "expert", turn(hop)) for hop in range(1, n_rows)]
        here = chunk
        if slot < n_donor - 1:
            chunk = lax.ppermute(chunk, "donor", rotation(n_donor, 1))
            chunk, gots, other_rows[:-1] = lax.optimization_barrier((chunk, gots, other_rows[:-1]))
        if slot == n_donor - 1 and slot > 0:
            gots, own_act[:slot], other_act[:slot] = lax.optimization_barrier(
                (gots, own_act[:slot], other_act[:slot])
            )
        if n_rows == 2:
            pieces = [jnp.where(y == 0, here, gots[0]), jnp.where(y == 0, gots[0], here)]
        else:
            stacked = jnp.stack([here] + gots, axis=0)
            pieces = [pick(stacked, (y - row) % n_rows) for row in range(n_rows)]
        block = jnp.concatenate(pieces, axis=1)
        resid_parts[slot] = lax.dynamic_slice_in_dim(block, z * columns, columns, 1)
        pieces = [piece.astype(f32) for piece in pieces]
        squares = sum(jnp.sum(piece * piece, axis=1, keepdims=True) for piece in pieces)
        inverse = lax.rsqrt(squares / model_width + 1e-06)
        normed = jnp.stack(
            [
                (piece * inverse * gain_f[None, row * pair_cols : (row + 1) * pair_cols]).astype(bf16)
                for row, piece in enumerate(pieces)
            ],
            axis=0,
        )
        own_rows.append(normed)
        other_rows.append(lax.ppermute(normed, "expert", swap))
        row_gates.append((pick(own_gates, part), pick(other_gates, part)))
        if len(row_gates) == batches[0]:
            batch = batches.pop(0)
            scale = jnp.concatenate([g[0] for g in row_gates] + [g[1] for g in row_gates])
            gate_up = sum(
                jnp.dot(
                    jnp.concatenate([rows[row] for rows in own_rows + other_rows], axis=0),
                    gate_up_weight[row * pair_cols : (row + 1) * pair_cols],
                    preferred_element_type=f32,
                )
                for row in range(n_rows)
            )
            act = jax.nn.silu(gate_up[:, :ff_local]) * gate_up[:, ff_local:]
            act = (act * scale[:, None]).astype(bf16).reshape(2, batch, part_rows, ff_local)
            for i in range(batch):
                own_act[slot - batch + 1 + i] = act[0, i]
                other_act[slot - batch + 1 + i] = act[1, i]
            own_rows, other_rows, row_gates = [], [], []

    def by_sequence(parts, rows):
        stacked = jnp.stack(parts, axis=0)
        return jnp.concatenate(
            [
                pick(stacked, (z - (y + r) % n_rows * parts_per_seq - i) % n_donor)
                for r in range(rows)
                for i in range(parts_per_seq)
            ],
            axis=0,
        )

    act_rows = jnp.concatenate(
        [by_sequence(other_act, n_rows), by_sequence(own_act, n_rows)], axis=0
    )
    half_rows = n_rows * suffix_len
    resid = by_sequence(resid_parts, 1).astype(f32)

    order = steps[::-1] + [0]
    pending, before = [], []
    for place, step in enumerate(order):
        if place == 2:
            act_rows = after(act_rows, *pending[0][1])
        down = lax.dynamic_slice_in_dim(w_down[0], (z + step) % n_donor * columns, columns, 1)
        mixed = jnp.dot(act_rows, down, preferred_element_type=f32)
        got = lax.ppermute(mixed[:half_rows].astype(bf16), "expert", swap)
        block = mixed[half_rows:] + after(got, *before).astype(f32)
        before = [block]
        block = block.reshape(n_rows, suffix_len, columns)
        arriving = [
            lax.ppermute(block[hop].astype(bf16), "expert", turn(hop)) for hop in range(1, n_rows)
        ]
        pending.append((block[0], arriving))
    total = resid
    carry = {1: [], -1: []}
    all_blocks, before = before, []
    for place, step in enumerate(order):
        part_sum, arriving = pending[place]
        part_sum = after(part_sum, *before)
        for got in arriving:
            part_sum = part_sum + got.astype(f32)
        before = [part_sum] + all_blocks
        if step:
            way = 1 if step <= n_donor // 2 else -1
            for got in carry[way]:
                part_sum = part_sum + got.astype(f32)
            carry[way] = [lax.ppermute(part_sum.astype(bf16), "donor", rotation(n_donor, way))]
        else:
            total = total + part_sum
    for got in carry[1] + carry[-1]:
        total = total + got.astype(f32)
    return (total.astype(bf16), head_out)


def solution(mesh):
    in_specs = (
        P(("groups", "expert"), None),
        P(("groups", "expert"), "donor"),
        P(("groups", "expert"), None, None),
        P(("groups", "expert", "donor"), None, None, None),
        P("groups", None),
        P("groups"),
        P("donor", "expert"),
        P(),
        P(("groups", "expert"), None),
        P(("groups", "expert"), None),
        P(("expert", "donor"), None, None, None),
        P(("expert", "donor"), None, None),
    )
    out_specs = (P(("groups", "expert"), "donor"), P(("groups", "expert"), "donor"))
    return jax.shard_map(shards, mesh=mesh, in_specs=in_specs, out_specs=out_specs, check_vma=False)
```

```python
import jax
import jax.numpy as jnp
from jax import lax
from jax.sharding import PartitionSpec as P


def rotation(count, step):
    return [(i, (i + step) % count) for i in range(count)]


def pick(array, index, axis=0):
    return lax.dynamic_index_in_dim(array, index, axis, keepdims=False)


def after(array, *others):
    return lax.optimization_barrier((array, *others))[0]


def attention(queries, suffix_kv, kv_pool, page_table, prefix_len):
    n_expert = lax.axis_size("expert")
    n_donor = lax.axis_size("donor")
    expert_index = lax.axis_index("expert")
    donor_index = lax.axis_index("donor")
    seq_count, page_count = page_table.shape
    suffix_len = queries.shape[0]
    kv_heads = suffix_kv.shape[1]
    head_dim = suffix_kv.shape[2] // 2
    page_len = kv_pool.shape[2]
    my_group = donor_index * kv_heads // n_donor
    owner_index = expert_index * n_donor + donor_index
    owner_of = page_table // seq_count
    held_slot = jnp.sum(jnp.where(owner_of == owner_index, page_table % seq_count, 0), axis=1)
    dest_group = jnp.arange(n_donor, dtype=jnp.int32) * kv_heads // n_donor
    wanted = (held_slot[:, None] * kv_heads + dest_group[None, :]).reshape(-1)
    outgoing = jnp.take(
        kv_pool.reshape(seq_count * kv_heads, page_len, 2 * head_dim), wanted, axis=0
    )
    arrived = lax.all_to_all(outgoing, ("expert", "donor"), split_axis=0, concat_axis=0, tiled=True)
    my_owners = lax.dynamic_index_in_dim(owner_of, expert_index, 0, keepdims=False)
    ordered = jnp.take(arrived, my_owners, axis=0).reshape(page_count * page_len, 2 * head_dim)
    prefix_keys = ordered[:, :head_dim]
    prefix_vals = ordered[:, head_dim:]
    score_scale = head_dim ** (-0.5)
    query_heads = queries.reshape(suffix_len, -1, head_dim)
    fresh_pair = lax.dynamic_index_in_dim(suffix_kv, my_group, 1, keepdims=False)
    causal = jnp.arange(suffix_len)[:, None] >= jnp.arange(suffix_len)[None, :]
    fresh_scores = (
        jnp.einsum(
            "thc,uc->thu", query_heads, fresh_pair[:, :head_dim], preferred_element_type=jnp.float32
        )
        * score_scale
    )
    fresh_scores = jnp.where(causal[:, None, :], fresh_scores, -jnp.inf)
    prefix_tokens = lax.dynamic_index_in_dim(prefix_len, expert_index, 0, keepdims=False)
    block_keys = min(1024, page_count * page_len)
    live_blocks = (prefix_tokens + block_keys - 1) // block_keys

    def block_scores(block_index):
        keys_block = lax.dynamic_slice_in_dim(prefix_keys, block_index * block_keys, block_keys, 0)
        raw_scores = (
            jnp.einsum("thc,kc->thk", query_heads, keys_block, preferred_element_type=jnp.float32)
            * score_scale
        )
        visible = block_index * block_keys + jnp.arange(block_keys) < prefix_tokens
        return jnp.where(visible[None, None, :], raw_scores, -jnp.inf)

    def raise_max(block_index, running):
        return jnp.maximum(running, jnp.max(block_scores(block_index), axis=2))

    row_max = lax.fori_loop(0, live_blocks, raise_max, jnp.max(fresh_scores, axis=2))

    def add_block(block_index, loop_state):
        row_total, weighted = loop_state
        exp_scores = jnp.exp(block_scores(block_index) - row_max[:, :, None])
        vals_block = lax.dynamic_slice_in_dim(prefix_vals, block_index * block_keys, block_keys, 0)
        weighted = weighted + jnp.einsum(
            "thk,kc->thc",
            exp_scores.astype(jnp.bfloat16),
            vals_block,
            preferred_element_type=jnp.float32,
        )
        return (row_total + jnp.sum(exp_scores, axis=2), weighted)

    fresh_exp = jnp.exp(fresh_scores - row_max[:, :, None])
    start_state = (
        jnp.sum(fresh_exp, axis=2),
        jnp.einsum(
            "thu,uc->thc",
            fresh_exp.astype(jnp.bfloat16),
            fresh_pair[:, head_dim:],
            preferred_element_type=jnp.float32,
        ),
    )
    row_total, weighted = lax.fori_loop(0, live_blocks, add_block, start_state)
    return (weighted / row_total[:, :, None]).astype(jnp.bfloat16).reshape(suffix_len, -1)


def shards(
    hidden_in,
    queries,
    suffix_kv,
    kv_pool,
    page_table,
    prefix_len,
    out_weight,
    norm_gain,
    expert_ids,
    route_probs,
    w_gate_up,
    w_down,
):
    f32, bf16 = jnp.float32, jnp.bfloat16
    n_expert = lax.axis_size("expert")
    n_donor = lax.axis_size("donor")
    expert_index = lax.axis_index("expert")
    z = lax.axis_index("donor")
    n_rows = n_expert // 2
    y = expert_index // 2
    core = expert_index % 2
    swap = [(i, i ^ 1) for i in range(n_expert)]

    def turn(step):
        return rotation(n_expert, 2 * step)

    suffix_len, model_width = hidden_in.shape
    experts_all = 2 * n_expert
    ff_local = w_gate_up.shape[3]
    share_count = n_donor // 2
    my_expert = 2 * expert_index + z // share_count
    pair_cols = model_width // n_rows
    part_rows = n_rows * suffix_len // n_donor
    parts_per_seq = suffix_len // part_rows
    columns = model_width // n_donor
    steps = sorted(range(1, n_donor), key=lambda step: min(step, n_donor - step))

    gates = route_probs / jnp.sum(route_probs, axis=1, keepdims=True)
    hits = expert_ids[:, :, None] == jnp.arange(experts_all, dtype=jnp.int32)
    gate_table = jnp.sum(jnp.where(hits, gates[:, :, None], 0.0), axis=1).T

    other_weight = lax.ppermute(out_weight, "expert", swap)

    part_owner = z * part_rows // suffix_len
    hidden_rows = lax.dynamic_slice_in_dim(hidden_in, z * part_rows % suffix_len, part_rows, 0)

    def hidden_block(row):
        return lax.dynamic_slice_in_dim(hidden_rows, row * pair_cols, pair_cols, 1)

    hidden_part = hidden_block(y)
    for step in range(1, n_rows):
        got = lax.ppermute(hidden_block((y + step) % n_rows), "expert", turn(step))
        hidden_part = jnp.where((y - step) % n_rows == part_owner, got, hidden_part)

    head_out = attention(queries, suffix_kv, kv_pool, page_table, prefix_len)
    gate_table = after(gate_table, head_out)
    tables = [gate_table] + [
        lax.ppermute(gate_table, "expert", rotation(n_expert, step)) for step in range(1, n_expert)
    ]

    heads = jnp.zeros((n_rows, suffix_len, head_out.shape[1]), bf16)
    heads = lax.dynamic_update_index_in_dim(heads, head_out, y, 0)
    for step in range(1, n_rows):
        got = lax.ppermute(head_out, "expert", turn(step))
        got, tables = lax.optimization_barrier((got, tables))
        heads = lax.dynamic_update_index_in_dim(heads, got, (y - step) % n_rows, 0)
    heads = heads.reshape(n_donor, part_rows, -1)
    heads = jnp.concatenate([pick(heads, (z + step) % n_donor) for step in range(n_donor)])
    own_terms = jnp.dot(heads, out_weight, preferred_element_type=f32)
    other_terms = jnp.dot(heads, other_weight, preferred_element_type=f32)

    def term(step):
        rows = slice(step * part_rows, (step + 1) * part_rows)
        own, other = own_terms[rows], other_terms[rows]
        return jnp.concatenate(
            [jnp.where(core == 0, own, other), jnp.where(core == 0, other, own)], axis=1
        )

    own_terms, other_terms, w_gate_up = lax.optimization_barrier(
        (own_terms, other_terms, w_gate_up)
    )
    gate_up_weight = w_gate_up[0].reshape(model_width, 2 * ff_local)
    gots = [
        lax.ppermute(term(step).astype(bf16), "donor", rotation(n_donor, step)) for step in steps
    ]
    gots, gate_up_weight = lax.optimization_barrier((gots, gate_up_weight))
    total = term(0) + hidden_part.astype(f32)
    for got in gots:
        total = total + got.astype(f32)
    chunk = total.astype(bf16)

    all_gates = jnp.stack([pick(table, my_expert) for table in tables], axis=0)

    def core_gates(which):
        rows = [pick(all_gates, (expert_index - 2 * r - which) % n_expert) for r in range(n_rows)]
        return jnp.concatenate(rows).reshape(n_donor, part_rows)

    own_gates, other_gates = core_gates(core), core_gates(1 - core)

    gain_f = norm_gain.astype(f32)
    resid_parts = [None] * n_donor
    own_act, other_act = [None] * n_donor, [None] * n_donor
    batches = [n_donor // 2, n_donor - n_donor // 2]
    own_rows, other_rows, row_gates = [], [], []
    for slot in range(n_donor):
        part = (z - slot) % n_donor
        gots = [lax.ppermute(chunk, "expert", turn(hop)) for hop in range(1, n_rows)]
        here = chunk
        if slot < n_donor - 1:
            chunk = lax.ppermute(chunk, "donor", rotation(n_donor, 1))
            chunk, gots, other_rows[:-1] = lax.optimization_barrier((chunk, gots, other_rows[:-1]))
        if slot == n_donor - 1 and slot > 0:
            gots, own_act[:slot], other_act[:slot] = lax.optimization_barrier(
                (gots, own_act[:slot], other_act[:slot])
            )
        if n_rows == 2:
            pieces = [jnp.where(y == 0, here, gots[0]), jnp.where(y == 0, gots[0], here)]
        else:
            stacked = jnp.stack([here] + gots, axis=0)
            pieces = [pick(stacked, (y - row) % n_rows) for row in range(n_rows)]
        block = jnp.concatenate(pieces, axis=1)
        resid_parts[slot] = lax.dynamic_slice_in_dim(block, z * columns, columns, 1)
        pieces = [piece.astype(f32) for piece in pieces]
        squares = sum(jnp.sum(piece * piece, axis=1, keepdims=True) for piece in pieces)
        inverse = lax.rsqrt(squares / model_width + 1e-06)
        normed = jnp.stack(
            [
                (piece * inverse * gain_f[None, row * pair_cols : (row + 1) * pair_cols]).astype(bf16)
                for row, piece in enumerate(pieces)
            ],
            axis=0,
        )
        own_rows.append(normed)
        other_rows.append(lax.ppermute(normed, "expert", swap))
        row_gates.append((pick(own_gates, part), pick(other_gates, part)))
        if len(row_gates) == batches[0]:
            batch = batches.pop(0)
            scale = jnp.concatenate([g[0] for g in row_gates] + [g[1] for g in row_gates])
            gate_up = sum(
                jnp.dot(
                    jnp.concatenate([rows[row] for rows in own_rows + other_rows], axis=0),
                    gate_up_weight[row * pair_cols : (row + 1) * pair_cols],
                    preferred_element_type=f32,
                )
                for row in range(n_rows)
            )
            act = jax.nn.silu(gate_up[:, :ff_local]) * gate_up[:, ff_local:]
            act = (act * scale[:, None]).astype(bf16).reshape(2, batch, part_rows, ff_local)
            for i in range(batch):
                own_act[slot - batch + 1 + i] = act[0, i]
                other_act[slot - batch + 1 + i] = act[1, i]
            own_rows, other_rows, row_gates = [], [], []

    def by_sequence(parts, rows):
        stacked = jnp.stack(parts, axis=0)
        return jnp.concatenate(
            [
                pick(stacked, (z - (y + r) % n_rows * parts_per_seq - i) % n_donor)
                for r in range(rows)
                for i in range(parts_per_seq)
            ],
            axis=0,
        )

    act_rows = jnp.concatenate(
        [by_sequence(other_act, n_rows), by_sequence(own_act, n_rows)], axis=0
    )
    half_rows = n_rows * suffix_len
    resid = by_sequence(resid_parts, 1).astype(f32)

    order = steps[::-1] + [0]
    pending, before = [], []
    for place, step in enumerate(order):
        if place == 2:
            act_rows = after(act_rows, *pending[0][1])
        down = lax.dynamic_slice_in_dim(w_down[0], (z + step) % n_donor * columns, columns, 1)
        mixed = jnp.dot(act_rows, down, preferred_element_type=f32)
        got = lax.ppermute(mixed[:half_rows].astype(bf16), "expert", swap)
        block = mixed[half_rows:] + after(got, *before).astype(f32)
        before = [block]
        block = block.reshape(n_rows, suffix_len, columns)
        arriving = [
            lax.ppermute(block[hop].astype(bf16), "expert", turn(hop)) for hop in range(1, n_rows)
        ]
        pending.append((block[0], arriving))
    total = resid
    carry = {1: [], -1: []}
    all_blocks, before = before, []
    for place, step in enumerate(order):
        part_sum, arriving = pending[place]
        part_sum = after(part_sum, *before)
        for got in arriving:
            part_sum = part_sum + got.astype(f32)
        before = [part_sum] + all_blocks
        if step:
            way = 1 if step <= n_donor // 2 else -1
            for got in carry[way]:
                part_sum = part_sum + got.astype(f32)
            carry[way] = [lax.ppermute(part_sum.astype(bf16), "donor", rotation(n_donor, way))]
        else:
            total = total + part_sum
    for got in carry[1] + carry[-1]:
        total = total + got.astype(f32)
    return (total.astype(bf16), head_out)


def solution(mesh):
    in_specs = (
        P(("groups", "expert"), None),
        P(("groups", "expert"), "donor"),
        P(("groups", "expert"), None, None),
        P(("groups", "expert", "donor"), None, None, None),
        P("groups", None),
        P("groups"),
        P("donor", "expert"),
        P(),
        P(("groups", "expert"), None),
        P(("groups", "expert"), None),
        P(("expert", "donor"), None, None, None),
        P(("expert", "donor"), None, None),
    )
    out_specs = (P(("groups", "expert"), "donor"), P(("groups", "expert"), "donor"))
    return jax.shard_map(shards, mesh=mesh, in_specs=in_specs, out_specs=out_specs, check_vma=False)
```

```python
import jax
import jax.numpy as jnp
from jax import lax
from jax.sharding import PartitionSpec as P


def rotation(count, step):
    return [(i, (i + step) % count) for i in range(count)]


def pick(array, index, axis=0):
    return lax.dynamic_index_in_dim(array, index, axis, keepdims=False)


def after(array, *others):
    return lax.optimization_barrier((array, *others))[0]


def attention(queries, suffix_kv, kv_pool, page_table, prefix_len):
    n_expert = lax.axis_size("expert")
    n_donor = lax.axis_size("donor")
    expert_index = lax.axis_index("expert")
    donor_index = lax.axis_index("donor")
    seq_count, page_count = page_table.shape
    suffix_len = queries.shape[0]
    kv_heads = suffix_kv.shape[1]
    head_dim = suffix_kv.shape[2] // 2
    page_len = kv_pool.shape[2]
    my_group = donor_index * kv_heads // n_donor
    owner_index = expert_index * n_donor + donor_index
    owner_of = page_table // seq_count
    held_slot = jnp.sum(jnp.where(owner_of == owner_index, page_table % seq_count, 0), axis=1)
    dest_group = jnp.arange(n_donor, dtype=jnp.int32) * kv_heads // n_donor
    wanted = (held_slot[:, None] * kv_heads + dest_group[None, :]).reshape(-1)
    outgoing = jnp.take(
        kv_pool.reshape(seq_count * kv_heads, page_len, 2 * head_dim), wanted, axis=0
    )
    arrived = lax.all_to_all(outgoing, ("expert", "donor"), split_axis=0, concat_axis=0, tiled=True)
    my_owners = lax.dynamic_index_in_dim(owner_of, expert_index, 0, keepdims=False)
    ordered = jnp.take(arrived, my_owners, axis=0).reshape(page_count * page_len, 2 * head_dim)
    prefix_keys = ordered[:, :head_dim]
    prefix_vals = ordered[:, head_dim:]
    score_scale = head_dim ** (-0.5)
    query_heads = queries.reshape(suffix_len, -1, head_dim)
    fresh_pair = lax.dynamic_index_in_dim(suffix_kv, my_group, 1, keepdims=False)
    causal = jnp.arange(suffix_len)[:, None] >= jnp.arange(suffix_len)[None, :]
    fresh_scores = (
        jnp.einsum(
            "thc,uc->thu", query_heads, fresh_pair[:, :head_dim], preferred_element_type=jnp.float32
        )
        * score_scale
    )
    fresh_scores = jnp.where(causal[:, None, :], fresh_scores, -jnp.inf)
    prefix_tokens = lax.dynamic_index_in_dim(prefix_len, expert_index, 0, keepdims=False)
    block_keys = min(1024, page_count * page_len)
    live_blocks = (prefix_tokens + block_keys - 1) // block_keys

    def block_scores(block_index):
        keys_block = lax.dynamic_slice_in_dim(prefix_keys, block_index * block_keys, block_keys, 0)
        raw_scores = (
            jnp.einsum("thc,kc->thk", query_heads, keys_block, preferred_element_type=jnp.float32)
            * score_scale
        )
        visible = block_index * block_keys + jnp.arange(block_keys) < prefix_tokens
        return jnp.where(visible[None, None, :], raw_scores, -jnp.inf)

    def raise_max(block_index, running):
        return jnp.maximum(running, jnp.max(block_scores(block_index), axis=2))

    row_max = lax.fori_loop(0, live_blocks, raise_max, jnp.max(fresh_scores, axis=2))

    def add_block(block_index, loop_state):
        row_total, weighted = loop_state
        exp_scores = jnp.exp(block_scores(block_index) - row_max[:, :, None])
        vals_block = lax.dynamic_slice_in_dim(prefix_vals, block_index * block_keys, block_keys, 0)
        weighted = weighted + jnp.einsum(
            "thk,kc->thc",
            exp_scores.astype(jnp.bfloat16),
            vals_block,
            preferred_element_type=jnp.float32,
        )
        return (row_total + jnp.sum(exp_scores, axis=2), weighted)

    fresh_exp = jnp.exp(fresh_scores - row_max[:, :, None])
    start_state = (
        jnp.sum(fresh_exp, axis=2),
        jnp.einsum(
            "thu,uc->thc",
            fresh_exp.astype(jnp.bfloat16),
            fresh_pair[:, head_dim:],
            preferred_element_type=jnp.float32,
        ),
    )
    row_total, weighted = lax.fori_loop(0, live_blocks, add_block, start_state)
    return (weighted / row_total[:, :, None]).astype(jnp.bfloat16).reshape(suffix_len, -1)


def shards(
    hidden_in,
    queries,
    suffix_kv,
    kv_pool,
    page_table,
    prefix_len,
    out_weight,
    norm_gain,
    expert_ids,
    route_probs,
    w_gate_up,
    w_down,
):
    f32, bf16 = jnp.float32, jnp.bfloat16
    n_expert = lax.axis_size("expert")
    n_donor = lax.axis_size("donor")
    expert_index = lax.axis_index("expert")
    z = lax.axis_index("donor")
    n_rows = n_expert // 2
    y = expert_index // 2
    core = expert_index % 2
    swap = [(i, i ^ 1) for i in range(n_expert)]

    def turn(step):
        return rotation(n_expert, 2 * step)

    suffix_len, model_width = hidden_in.shape
    experts_all = 2 * n_expert
    ff_local = w_gate_up.shape[3]
    share_count = n_donor // 2
    my_expert = 2 * expert_index + z // share_count
    pair_cols = model_width // n_rows
    part_rows = n_rows * suffix_len // n_donor
    parts_per_seq = suffix_len // part_rows
    columns = model_width // n_donor
    steps = sorted(range(1, n_donor), key=lambda step: min(step, n_donor - step))

    gates = route_probs / jnp.sum(route_probs, axis=1, keepdims=True)
    hits = expert_ids[:, :, None] == jnp.arange(experts_all, dtype=jnp.int32)
    gate_table = jnp.sum(jnp.where(hits, gates[:, :, None], 0.0), axis=1).T

    other_weight = lax.ppermute(out_weight, "expert", swap)

    part_owner = z * part_rows // suffix_len
    hidden_rows = lax.dynamic_slice_in_dim(hidden_in, z * part_rows % suffix_len, part_rows, 0)

    def hidden_block(row):
        return lax.dynamic_slice_in_dim(hidden_rows, row * pair_cols, pair_cols, 1)

    hidden_part = hidden_block(y)
    for step in range(1, n_rows):
        got = lax.ppermute(hidden_block((y + step) % n_rows), "expert", turn(step))
        hidden_part = jnp.where((y - step) % n_rows == part_owner, got, hidden_part)

    head_out = attention(queries, suffix_kv, kv_pool, page_table, prefix_len)
    gate_table = after(gate_table, head_out)
    tables = [gate_table] + [
        lax.ppermute(gate_table, "expert", rotation(n_expert, step)) for step in range(1, n_expert)
    ]

    heads = jnp.zeros((n_rows, suffix_len, head_out.shape[1]), bf16)
    heads = lax.dynamic_update_index_in_dim(heads, head_out, y, 0)
    for step in range(1, n_rows):
        got = lax.ppermute(head_out, "expert", turn(step))
        got, tables = lax.optimization_barrier((got, tables))
        heads = lax.dynamic_update_index_in_dim(heads, got, (y - step) % n_rows, 0)
    heads = heads.reshape(n_donor, part_rows, -1)
    heads = jnp.concatenate([pick(heads, (z + step) % n_donor) for step in range(n_donor)])
    own_terms = jnp.dot(heads, out_weight, preferred_element_type=f32)
    other_terms = jnp.dot(heads, other_weight, preferred_element_type=f32)

    def term(step):
        rows = slice(step * part_rows, (step + 1) * part_rows)
        own, other = own_terms[rows], other_terms[rows]
        return jnp.concatenate(
            [jnp.where(core == 0, own, other), jnp.where(core == 0, other, own)], axis=1
        )

    w_gate_up = after(w_gate_up, own_terms[:1, :1], other_terms[:1, :1])
    gate_up_weight = w_gate_up[0].reshape(model_width, 2 * ff_local)
    gots = [
        lax.ppermute(term(step).astype(bf16), "donor", rotation(n_donor, step)) for step in steps
    ]
    gots, gate_up_weight = lax.optimization_barrier((gots, gate_up_weight))
    total = term(0) + hidden_part.astype(f32)
    for got in gots:
        total = total + got.astype(f32)
    chunk = total.astype(bf16)

    all_gates = jnp.stack([pick(table, my_expert) for table in tables], axis=0)

    def core_gates(which):
        rows = [pick(all_gates, (expert_index - 2 * r - which) % n_expert) for r in range(n_rows)]
        return jnp.concatenate(rows).reshape(n_donor, part_rows)

    own_gates, other_gates = core_gates(core), core_gates(1 - core)

    gain_f = norm_gain.astype(f32)
    resid_parts = [None] * n_donor
    own_act, other_act = [None] * n_donor, [None] * n_donor
    batches = [n_donor // 2, n_donor - n_donor // 2]
    own_rows, other_rows, row_gates = [], [], []
    for slot in range(n_donor):
        part = (z - slot) % n_donor
        gots = [lax.ppermute(chunk, "expert", turn(hop)) for hop in range(1, n_rows)]
        here = chunk
        if slot < n_donor - 1:
            chunk = lax.ppermute(chunk, "donor", rotation(n_donor, 1))
            chunk, gots, other_rows[:-1] = lax.optimization_barrier((chunk, gots, other_rows[:-1]))
        if slot == n_donor - 1 and slot > 0:
            gots, own_act[:slot], other_act[:slot] = lax.optimization_barrier(
                (gots, own_act[:slot], other_act[:slot])
            )
        if n_rows == 2:
            pieces = [jnp.where(y == 0, here, gots[0]), jnp.where(y == 0, gots[0], here)]
        else:
            stacked = jnp.stack([here] + gots, axis=0)
            pieces = [pick(stacked, (y - row) % n_rows) for row in range(n_rows)]
        block = jnp.concatenate(pieces, axis=1)
        resid_parts[slot] = lax.dynamic_slice_in_dim(block, z * columns, columns, 1)
        pieces = [piece.astype(f32) for piece in pieces]
        squares = sum(jnp.sum(piece * piece, axis=1, keepdims=True) for piece in pieces)
        inverse = lax.rsqrt(squares / model_width + 1e-06)
        normed = jnp.stack(
            [
                (piece * inverse * gain_f[None, row * pair_cols : (row + 1) * pair_cols]).astype(bf16)
                for row, piece in enumerate(pieces)
            ],
            axis=0,
        )
        own_rows.append(normed)
        other_rows.append(lax.ppermute(normed, "expert", swap))
        row_gates.append((pick(own_gates, part), pick(other_gates, part)))
        if len(row_gates) == batches[0]:
            batch = batches.pop(0)
            scale = jnp.concatenate([g[0] for g in row_gates] + [g[1] for g in row_gates])
            gate_up = sum(
                jnp.dot(
                    jnp.concatenate([rows[row] for rows in own_rows + other_rows], axis=0),
                    gate_up_weight[row * pair_cols : (row + 1) * pair_cols],
                    preferred_element_type=f32,
                )
                for row in range(n_rows)
            )
            act = jax.nn.silu(gate_up[:, :ff_local]) * gate_up[:, ff_local:]
            act = (act * scale[:, None]).astype(bf16).reshape(2, batch, part_rows, ff_local)
            for i in range(batch):
                own_act[slot - batch + 1 + i] = act[0, i]
                other_act[slot - batch + 1 + i] = act[1, i]
            own_rows, other_rows, row_gates = [], [], []

    def by_sequence(parts, rows):
        stacked = jnp.stack(parts, axis=0)
        return jnp.concatenate(
            [
                pick(stacked, (z - (y + r) % n_rows * parts_per_seq - i) % n_donor)
                for r in range(rows)
                for i in range(parts_per_seq)
            ],
            axis=0,
        )

    act_rows = jnp.concatenate(
        [by_sequence(other_act, n_rows), by_sequence(own_act, n_rows)], axis=0
    )
    half_rows = n_rows * suffix_len
    resid = by_sequence(resid_parts, 1).astype(f32)

    order = steps[::-1] + [0]
    pending, before = [], []
    for place, step in enumerate(order):
        if place == 2:
            act_rows = after(act_rows, *pending[0][1])
        down = lax.dynamic_slice_in_dim(w_down[0], (z + step) % n_donor * columns, columns, 1)
        mixed = jnp.dot(act_rows, down, preferred_element_type=f32)
        got = lax.ppermute(mixed[:half_rows].astype(bf16), "expert", swap)
        block = mixed[half_rows:] + after(got, *before).astype(f32)
        before = [block]
        block = block.reshape(n_rows, suffix_len, columns)
        arriving = [
            lax.ppermute(block[hop].astype(bf16), "expert", turn(hop)) for hop in range(1, n_rows)
        ]
        pending.append((block[0], arriving))
    total = resid
    carry = {1: [], -1: []}
    all_blocks, before = before, []
    for place, step in enumerate(order):
        part_sum, arriving = pending[place]
        part_sum = after(part_sum, *before)
        for got in arriving:
            part_sum = part_sum + got.astype(f32)
        before = [part_sum] + all_blocks
        if step:
            way = 1 if step <= n_donor // 2 else -1
            for got in carry[way]:
                part_sum = part_sum + got.astype(f32)
            carry[way] = [lax.ppermute(part_sum.astype(bf16), "donor", rotation(n_donor, way))]
        else:
            total = total + part_sum
    for got in carry[1] + carry[-1]:
        total = total + got.astype(f32)
    return (total.astype(bf16), head_out)


def solution(mesh):
    in_specs = (
        P(("groups", "expert"), None),
        P(("groups", "expert"), "donor"),
        P(("groups", "expert"), None, None),
        P(("groups", "expert", "donor"), None, None, None),
        P("groups", None),
        P("groups"),
        P("donor", "expert"),
        P(),
        P(("groups", "expert"), None),
        P(("groups", "expert"), None),
        P(("expert", "donor"), None, None, None),
        P(("expert", "donor"), None, None),
    )
    out_specs = (P(("groups", "expert"), "donor"), P(("groups", "expert"), "donor"))
    return jax.shard_map(shards, mesh=mesh, in_specs=in_specs, out_specs=out_specs, check_vma=False)
```

```python
import jax
import jax.numpy as jnp
from jax import lax
from jax.sharding import PartitionSpec as P


def rotation(count, step):
    return [(i, (i + step) % count) for i in range(count)]


def pick(array, index, axis=0):
    return lax.dynamic_index_in_dim(array, index, axis, keepdims=False)


def after(array, *others):
    return lax.optimization_barrier((array, *others))[0]


def attention(queries, suffix_kv, kv_pool, page_table, prefix_len):
    n_expert = lax.axis_size("expert")
    n_donor = lax.axis_size("donor")
    expert_index = lax.axis_index("expert")
    donor_index = lax.axis_index("donor")
    seq_count, page_count = page_table.shape
    suffix_len = queries.shape[0]
    kv_heads = suffix_kv.shape[1]
    head_dim = suffix_kv.shape[2] // 2
    page_len = kv_pool.shape[2]
    my_group = donor_index * kv_heads // n_donor
    owner_index = expert_index * n_donor + donor_index
    owner_of = page_table // seq_count
    held_slot = jnp.sum(jnp.where(owner_of == owner_index, page_table % seq_count, 0), axis=1)
    dest_group = jnp.arange(n_donor, dtype=jnp.int32) * kv_heads // n_donor
    wanted = (held_slot[:, None] * kv_heads + dest_group[None, :]).reshape(-1)
    outgoing = jnp.take(
        kv_pool.reshape(seq_count * kv_heads, page_len, 2 * head_dim), wanted, axis=0
    )
    arrived = lax.all_to_all(outgoing, ("expert", "donor"), split_axis=0, concat_axis=0, tiled=True)
    my_owners = lax.dynamic_index_in_dim(owner_of, expert_index, 0, keepdims=False)
    ordered = jnp.take(arrived, my_owners, axis=0).reshape(page_count * page_len, 2 * head_dim)
    prefix_keys = ordered[:, :head_dim]
    prefix_vals = ordered[:, head_dim:]
    score_scale = head_dim ** (-0.5)
    query_heads = queries.reshape(suffix_len, -1, head_dim)
    fresh_pair = lax.dynamic_index_in_dim(suffix_kv, my_group, 1, keepdims=False)
    causal = jnp.arange(suffix_len)[:, None] >= jnp.arange(suffix_len)[None, :]
    fresh_scores = (
        jnp.einsum(
            "thc,uc->thu", query_heads, fresh_pair[:, :head_dim], preferred_element_type=jnp.float32
        )
        * score_scale
    )
    fresh_scores = jnp.where(causal[:, None, :], fresh_scores, -jnp.inf)
    prefix_tokens = lax.dynamic_index_in_dim(prefix_len, expert_index, 0, keepdims=False)
    block_keys = min(1024, page_count * page_len)
    live_blocks = (prefix_tokens + block_keys - 1) // block_keys

    def block_scores(block_index):
        keys_block = lax.dynamic_slice_in_dim(prefix_keys, block_index * block_keys, block_keys, 0)
        raw_scores = (
            jnp.einsum("thc,kc->thk", query_heads, keys_block, preferred_element_type=jnp.float32)
            * score_scale
        )
        visible = block_index * block_keys + jnp.arange(block_keys) < prefix_tokens
        return jnp.where(visible[None, None, :], raw_scores, -jnp.inf)

    def raise_max(block_index, running):
        return jnp.maximum(running, jnp.max(block_scores(block_index), axis=2))

    row_max = lax.fori_loop(0, live_blocks, raise_max, jnp.max(fresh_scores, axis=2))

    def add_block(block_index, loop_state):
        row_total, weighted = loop_state
        exp_scores = jnp.exp(block_scores(block_index) - row_max[:, :, None])
        vals_block = lax.dynamic_slice_in_dim(prefix_vals, block_index * block_keys, block_keys, 0)
        weighted = weighted + jnp.einsum(
            "thk,kc->thc",
            exp_scores.astype(jnp.bfloat16),
            vals_block,
            preferred_element_type=jnp.float32,
        )
        return (row_total + jnp.sum(exp_scores, axis=2), weighted)

    fresh_exp = jnp.exp(fresh_scores - row_max[:, :, None])
    start_state = (
        jnp.sum(fresh_exp, axis=2),
        jnp.einsum(
            "thu,uc->thc",
            fresh_exp.astype(jnp.bfloat16),
            fresh_pair[:, head_dim:],
            preferred_element_type=jnp.float32,
        ),
    )
    row_total, weighted = lax.fori_loop(0, live_blocks, add_block, start_state)
    return (weighted / row_total[:, :, None]).astype(jnp.bfloat16).reshape(suffix_len, -1)


def shards(
    hidden_in,
    queries,
    suffix_kv,
    kv_pool,
    page_table,
    prefix_len,
    out_weight,
    norm_gain,
    expert_ids,
    route_probs,
    w_gate_up,
    w_down,
):
    f32, bf16 = jnp.float32, jnp.bfloat16
    n_expert = lax.axis_size("expert")
    n_donor = lax.axis_size("donor")
    expert_index = lax.axis_index("expert")
    z = lax.axis_index("donor")
    n_rows = n_expert // 2
    y = expert_index // 2
    core = expert_index % 2
    swap = [(i, i ^ 1) for i in range(n_expert)]

    def turn(step):
        return rotation(n_expert, 2 * step)

    suffix_len, model_width = hidden_in.shape
    experts_all = 2 * n_expert
    ff_local = w_gate_up.shape[3]
    share_count = n_donor // 2
    my_expert = 2 * expert_index + z // share_count
    pair_cols = model_width // n_rows
    part_rows = n_rows * suffix_len // n_donor
    parts_per_seq = suffix_len // part_rows
    columns = model_width // n_donor
    steps = sorted(range(1, n_donor), key=lambda step: min(step, n_donor - step))

    gates = route_probs / jnp.sum(route_probs, axis=1, keepdims=True)
    hits = expert_ids[:, :, None] == jnp.arange(experts_all, dtype=jnp.int32)
    gate_table = jnp.sum(jnp.where(hits, gates[:, :, None], 0.0), axis=1).T

    other_weight = lax.ppermute(out_weight, "expert", swap)

    part_owner = z * part_rows // suffix_len
    hidden_rows = lax.dynamic_slice_in_dim(hidden_in, z * part_rows % suffix_len, part_rows, 0)

    def hidden_block(row):
        return lax.dynamic_slice_in_dim(hidden_rows, row * pair_cols, pair_cols, 1)

    hidden_part = hidden_block(y)
    for step in range(1, n_rows):
        got = lax.ppermute(hidden_block((y + step) % n_rows), "expert", turn(step))
        hidden_part = jnp.where((y - step) % n_rows == part_owner, got, hidden_part)

    head_out = attention(queries, suffix_kv, kv_pool, page_table, prefix_len)
    gate_table = after(gate_table, head_out)
    tables = [gate_table] + [
        lax.ppermute(gate_table, "expert", rotation(n_expert, step)) for step in range(1, n_expert)
    ]

    heads = jnp.zeros((n_rows, suffix_len, head_out.shape[1]), bf16)
    heads = lax.dynamic_update_index_in_dim(heads, head_out, y, 0)
    for step in range(1, n_rows):
        got = lax.ppermute(head_out, "expert", turn(step))
        got, tables = lax.optimization_barrier((got, tables))
        heads = lax.dynamic_update_index_in_dim(heads, got, (y - step) % n_rows, 0)
    heads = heads.reshape(n_donor, part_rows, -1)
    heads = jnp.concatenate([pick(heads, (z + step) % n_donor) for step in range(n_donor)])
    own_terms = jnp.dot(heads, out_weight, preferred_element_type=f32)
    other_terms = jnp.dot(heads, other_weight, preferred_element_type=f32)

    def term(step):
        rows = slice(step * part_rows, (step + 1) * part_rows)
        own, other = own_terms[rows], other_terms[rows]
        return jnp.concatenate(
            [jnp.where(core == 0, own, other), jnp.where(core == 0, other, own)], axis=1
        )

    own_terms, other_terms, w_gate_up = lax.optimization_barrier(
        (own_terms, other_terms, w_gate_up)
    )
    gate_up_weight = w_gate_up[0].reshape(model_width, 2 * ff_local)
    gots = [
        lax.ppermute(term(step).astype(bf16), "donor", rotation(n_donor, step)) for step in steps
    ]
    gots, gate_up_weight = lax.optimization_barrier((gots, gate_up_weight))
    total = term(0) + hidden_part.astype(f32)
    for got in gots:
        total = total + got.astype(f32)
    chunk = total.astype(bf16)

    all_gates = jnp.stack([pick(table, my_expert) for table in tables], axis=0)

    def core_gates(which):
        rows = [pick(all_gates, (expert_index - 2 * r - which) % n_expert) for r in range(n_rows)]
        return jnp.concatenate(rows).reshape(n_donor, part_rows)

    own_gates, other_gates = core_gates(core), core_gates(1 - core)

    gain_f = norm_gain.astype(f32)
    resid_parts = [None] * n_donor
    own_act, other_act = [None] * n_donor, [None] * n_donor
    batches = [max(1, n_donor - 1), 1]
    own_rows, other_rows, row_gates = [], [], []
    for slot in range(n_donor):
        part = (z - slot) % n_donor
        gots = [lax.ppermute(chunk, "expert", turn(hop)) for hop in range(1, n_rows)]
        here = chunk
        if slot < n_donor - 1:
            chunk = lax.ppermute(chunk, "donor", rotation(n_donor, 1))
            chunk, gots, other_rows[:-1] = lax.optimization_barrier((chunk, gots, other_rows[:-1]))
        if slot == n_donor - 1 and slot > 0:
            gots, own_act[:slot], other_act[:slot] = lax.optimization_barrier(
                (gots, own_act[:slot], other_act[:slot])
            )
        if n_rows == 2:
            pieces = [jnp.where(y == 0, here, gots[0]), jnp.where(y == 0, gots[0], here)]
        else:
            stacked = jnp.stack([here] + gots, axis=0)
            pieces = [pick(stacked, (y - row) % n_rows) for row in range(n_rows)]
        block = jnp.concatenate(pieces, axis=1)
        resid_parts[slot] = lax.dynamic_slice_in_dim(block, z * columns, columns, 1)
        pieces = [piece.astype(f32) for piece in pieces]
        squares = sum(jnp.sum(piece * piece, axis=1, keepdims=True) for piece in pieces)
        inverse = lax.rsqrt(squares / model_width + 1e-06)
        normed = jnp.stack(
            [
                (piece * inverse * gain_f[None, row * pair_cols : (row + 1) * pair_cols]).astype(bf16)
                for row, piece in enumerate(pieces)
            ],
            axis=0,
        )
        own_rows.append(normed)
        other_rows.append(lax.ppermute(normed, "expert", swap))
        row_gates.append((pick(own_gates, part), pick(other_gates, part)))
        if len(row_gates) == batches[0]:
            batch = batches.pop(0)
            scale = jnp.concatenate([g[0] for g in row_gates] + [g[1] for g in row_gates])
            gate_up = sum(
                jnp.dot(
                    jnp.concatenate([rows[row] for rows in own_rows + other_rows], axis=0),
                    gate_up_weight[row * pair_cols : (row + 1) * pair_cols],
                    preferred_element_type=f32,
                )
                for row in range(n_rows)
            )
            act = jax.nn.silu(gate_up[:, :ff_local]) * gate_up[:, ff_local:]
            act = (act * scale[:, None]).astype(bf16).reshape(2, batch, part_rows, ff_local)
            for i in range(batch):
                own_act[slot - batch + 1 + i] = act[0, i]
                other_act[slot - batch + 1 + i] = act[1, i]
            own_rows, other_rows, row_gates = [], [], []

    def by_sequence(parts, rows):
        stacked = jnp.stack(parts, axis=0)
        return jnp.concatenate(
            [
                pick(stacked, (z - (y + r) % n_rows * parts_per_seq - i) % n_donor)
                for r in range(rows)
                for i in range(parts_per_seq)
            ],
            axis=0,
        )

    act_rows = jnp.concatenate(
        [by_sequence(other_act, n_rows), by_sequence(own_act, n_rows)], axis=0
    )
    half_rows = n_rows * suffix_len
    resid = by_sequence(resid_parts, 1).astype(f32)

    order = steps[::-1] + [0]
    pending, before = [], []
    for place, step in enumerate(order):
        if place == 2:
            act_rows = after(act_rows, *pending[0][1])
        down = lax.dynamic_slice_in_dim(w_down[0], (z + step) % n_donor * columns, columns, 1)
        mixed = jnp.dot(act_rows, down, preferred_element_type=f32)
        got = lax.ppermute(mixed[:half_rows].astype(bf16), "expert", swap)
        block = mixed[half_rows:] + after(got, *before).astype(f32)
        before = [block]
        block = block.reshape(n_rows, suffix_len, columns)
        arriving = [
            lax.ppermute(block[hop].astype(bf16), "expert", turn(hop)) for hop in range(1, n_rows)
        ]
        pending.append((block[0], arriving))
    total = resid
    carry = {1: [], -1: []}
    all_blocks, before = before, []
    for place, step in enumerate(order):
        part_sum, arriving = pending[place]
        part_sum = after(part_sum, *before)
        for got in arriving:
            part_sum = part_sum + got.astype(f32)
        before = [part_sum] + all_blocks
        if step:
            way = 1 if step <= n_donor // 2 else -1
            for got in carry[way]:
                part_sum = part_sum + got.astype(f32)
            carry[way] = [lax.ppermute(part_sum.astype(bf16), "donor", rotation(n_donor, way))]
        else:
            total = total + part_sum
    for got in carry[1] + carry[-1]:
        total = total + got.astype(f32)
    return (total.astype(bf16), head_out)


def solution(mesh):
    in_specs = (
        P(("groups", "expert"), None),
        P(("groups", "expert"), "donor"),
        P(("groups", "expert"), None, None),
        P(("groups", "expert", "donor"), None, None, None),
        P("groups", None),
        P("groups"),
        P("donor", "expert"),
        P(),
        P(("groups", "expert"), None),
        P(("groups", "expert"), None),
        P(("expert", "donor"), None, None, None),
        P(("expert", "donor"), None, None),
    )
    out_specs = (P(("groups", "expert"), "donor"), P(("groups", "expert"), "donor"))
    return jax.shard_map(shards, mesh=mesh, in_specs=in_specs, out_specs=out_specs, check_vma=False)
```
